32 devices in a mesh: groups: 2 (over x), req: 4 (over y, core), tp: 4 (over z).
Axes of the slice: x: 2, y: 2, z: 4, core: 2. Of those that a mesh axis runs over, the one named last changes fastest.
Arguments:
- ssm_input: bfloat16 [4096, 8192], P(('groups', 'req'), 'tp'), parts along dimension 0, may hold values from -6 to 6
- gate_input: bfloat16 [4096, 8192], P(('groups', 'req'), 'tp'), parts along dimension 0, may hold values from -6 to 6
- bc_input: bfloat16 [4096, 1024], P(('groups', 'req')), parts along dimension 0, may hold values from -6 to 6
- dt_input: float32 [4096, 128], P(('groups', 'req'), 'tp'), parts along dimension 0, may hold values from -6 to 6
- decay_rate: float32 [128], P('tp'), may hold values from 0.002 to 0.15
- skip_gain: float32 [128], P('tp'), may hold values from 0.5 to 1.5
- norm_gain: float32 [8192], P('tp'), may hold values from 0.1 to 1.9
- conv_x_weight: bfloat16 [4, 8192], P(None, 'tp'), may hold values from -3 to 3
- conv_bc_weight: bfloat16 [4, 1024], replicated, may hold values from -3 to 3
- out_weight: bfloat16 [8192, 4096], P('tp'), may hold values from -0.0625 to 0.0625
- pool_states: float32 [16, 128, 64, 128], P(('groups', 'req'), 'tp'), parts along dimension 0, may hold values from -24 to 24
- pool_conv_x: bfloat16 [16, 3, 8192], P(('groups', 'req'), None, 'tp'), parts along dimension 0, may hold values from -6 to 6
- pool_conv_bc: bfloat16 [16, 3, 1024], P(('groups', 'req')), parts along dimension 0, may hold values from -6 to 6
- prefix_slot: int32 [8], P('groups'), parts along dimension 0, may hold values from 0 to 7
- prefix_spans: int32 [8], P('groups'), parts along dimension 0, may hold values from 0 to 3
- dest_slot: int32 [8], P('groups'), parts along dimension 0, may hold values from 0 to 3, each once
- suffix_len: int32 [8], P('groups'), parts along dimension 0, may hold values from 1 to 512, 1280 in all
Outputs:
- mixed: bfloat16 [4096, 4096], P(('groups', 'req'), 'tp'), parts along dimension 0
- ckpt_states: float32 [8, 128, 64, 128], P(('groups', 'req'), 'tp'), parts along dimension 0
- ckpt_conv_x: bfloat16 [8, 3, 8192], P(('groups', 'req'), None, 'tp'), parts along dimension 0
- ckpt_conv_bc: bfloat16 [8, 3, 1024], P(('groups', 'req')), parts along dimension 0
The draws below stay inside these ranges and needn't reach their ends.
There are 2 independent parts, one for each index of `groups`. The reference program is written for one: setup_inputs(seed, part) draws one part's arguments, and reference() takes and returns one part's arrays. A program takes and returns all parts, laid end to end along the dimension named above; an argument that names none is the same for every part. Nothing has to cross between parts.
Inputs may be any that keep to these rules, and one draw needn't show every extreme that they name: `prefix_slot`: slot s of the pool lives on req index s // 2; several requests may share one slot. `prefix_spans`: 0 means the request has no cached prefix. `dest_slot`: all different; store slot s lives on req index s. `suffix_len`: they sum to 1280 and one equals 512.
All inputs are finite; a program needn't handle non-finite values.
Results may differ from the reference program's by a relative error of at most 0.012.
Values may be sent and summed in bfloat16 or wider, within the bound.
No kernel may reach another device: no remote copies, remote signals or barrier semaphores. Data moves between devices by JAX's collectives and lax.ppermute only.
A program may use at most 192 MiB of HBM per device.

```python
import math
import jax
import jax.numpy as jnp
import numpy as np
from jax import lax

D = 4096
HEADS = 128
HDIM = 64
STATE = 128
GHEADS = 32
CONV = 4
SPAN = 128
SUF = 512
INNER = 8192
BCG = 4
BCW = 1024
NCH = 4
REQUESTS = 4
POOL = 8
TOKENS = 2048
LIVE = 1280
N_TP = 4


def set_ends(drawn, rng, low, largest):
    longest = drawn.shape.index(max(drawn.shape))
    spots = []
    for shift in (0, 1):
        where = [jax.random.randint(jax.random.fold_in(rng, axis), (), 0, length) for axis, length in enumerate(drawn.shape)]
        where[longest] = (where[longest] + shift) % drawn.shape[longest]
        spots.append(tuple(where))
    return drawn.at[spots[0]].set(low).at[spots[1]].set(largest)


def levels(own_key, extent, pieces, smallest, top_value):
    gain, own = 1.0, jax.random.fold_in(own_key, 6)
    for axis_at, shards_of in pieces:
        steps = jnp.exp(jax.random.uniform(jax.random.fold_in(own, axis_at), (shards_of,), jnp.float32, smallest / len(pieces), top_value / len(pieces)))
        gain = gain * jnp.repeat(steps, extent[axis_at] // shards_of).reshape([-1 if axis == axis_at else 1 for axis in range(len(extent))])
    return gain


def rank_table(amount, skew):
    loads = [(1 << 20) // math.isqrt(standing ** skew) + 1 for standing in range(1, amount + 1)]
    scale = 1 + sum(loads) // (1 << 30)
    return np.cumsum(np.array([max(1, weight // scale) for weight in loads]))


def ranked(rng, extent, count, lean):
    table = rank_table(count, lean)
    lot = jax.random.randint(jax.random.fold_in(rng, 1), extent, 0, int(table[count - 1]))
    grade = jnp.searchsorted(jnp.asarray(table, jnp.int32), lot, side="right")
    return jax.random.permutation(jax.random.fold_in(rng, 2), count)[grade].astype(jnp.int32)


def length_profile(count, total, reach, skew):
    weights = [(1 << 20) // math.isqrt(standing ** skew) + 1 for standing in range(2, count + 1)]
    rest, counts = total - reach - (count - 1), [1] * (count - 1)
    while rest > 0:
        free = [i for i in range(count - 1) if counts[i] < reach]
        pool, remaining = sum([weights[i] for i in free]), rest
        for i in free:
            addition = min(reach - counts[i], max(1, remaining * weights[i] // pool), rest)
            counts[i] = counts[i] + addition
            rest = rest - addition
    return np.array([reach] + counts)


def uneven(rng, count, total, limit, skew):
    if count == 2:
        one = jax.random.randint(rng, (), max(1, total - limit), min(limit, total - 1) + 1)
        return jnp.stack([one, total - one])
    sizes = jnp.asarray(length_profile(count, total, limit, skew), jnp.int32)
    pairs = (count - 1) // 2
    giver, sink = sizes[1:1 + 2 * pairs:2], sizes[2:2 + 2 * pairs:2]
    slack = jnp.minimum(giver - 1, limit - sink)
    passed = jax.random.randint(jax.random.fold_in(rng, 1), (pairs,), 0, 1 << 20) % (slack + 1)
    sizes = sizes.at[1:1 + 2 * pairs:2].set(giver - passed).at[2:2 + 2 * pairs:2].set(sink + passed)
    return sizes[jax.random.permutation(jax.random.fold_in(rng, 2), count)]


def bell_draw(stream_key, dims, deviation, limit, pieces=(), held_as=jnp.bfloat16):
    array = deviation * jax.random.normal(stream_key, dims, jnp.float32)
    if pieces:
        array = array * levels(stream_key, dims, pieces, -0.22, 0.18)
    return jnp.clip(array, -limit, limit).astype(held_as)


def setup_inputs(seed: int = 0, part: int = 0) -> dict:
    streams_of = jax.random.split(jax.random.key(seed), 18)
    part_keys = jax.random.split(jax.random.fold_in(streams_of[17], part), 18)
    return {
        "ssm_input": bell_draw(part_keys[0], (TOKENS, INNER), 1.0, 6.0, ((0, 4), (1, 4))),
        "gate_input": bell_draw(part_keys[1], (TOKENS, INNER), 1.0, 6.0, ((0, 4), (1, 4))),
        "bc_input": bell_draw(part_keys[2], (TOKENS, BCW), 1.0, 6.0, ((0, 4),)),
        "dt_input": bell_draw(part_keys[3], (TOKENS, HEADS), 1.0, 6.0, ((0, 4), (1, 4)), jnp.float32),
        "decay_rate": jnp.clip(jnp.exp(math.log(0.15) - 4.317488 * jax.random.uniform(streams_of[4], (HEADS,), jnp.float32) ** levels(streams_of[4], (HEADS,), ((0, 4),), -0.2, 0.2)), 0.002, 0.15),
        "skip_gain": jnp.clip(0.5 + 1.0 * jax.random.uniform(streams_of[5], (HEADS,), jnp.float32) ** levels(streams_of[5], (HEADS,), ((0, 4),), -0.2, 0.2), 0.5, 1.5),
        "norm_gain": jnp.clip(1.0 + 0.18 * jax.random.normal(streams_of[6], (INNER,), jnp.float32), 0.1, 1.9),
        "conv_x_weight": bell_draw(streams_of[7], (CONV, INNER), CONV ** -0.5, 3.0, ((1, 4),)),
        "conv_bc_weight": bell_draw(streams_of[8], (CONV, BCW), CONV ** -0.5, 3.0),
        "out_weight": bell_draw(streams_of[9], (INNER, D), INNER ** -0.5, 0.0625, ((0, 4),)),
        "pool_states": bell_draw(part_keys[10], (POOL, HEADS, HDIM, STATE), 4.0, 24.0, ((0, 4), (1, 4)), jnp.float32),
        "pool_conv_x": bell_draw(part_keys[11], (POOL, CONV - 1, INNER), 1.0, 6.0, ((0, 4), (2, 4))),
        "pool_conv_bc": bell_draw(part_keys[12], (POOL, CONV - 1, BCW), 1.0, 6.0, ((0, 4),)),
        "prefix_slot": set_ends(ranked(part_keys[13], (REQUESTS,), POOL, 2), jax.random.fold_in(part_keys[13], 3), 0, POOL - 1).astype(jnp.int32),
        "prefix_spans": set_ends(jax.random.randint(part_keys[14], (REQUESTS,), 0, 4), jax.random.fold_in(part_keys[14], 1), 0, 3).astype(jnp.int32),
        "dest_slot": jax.random.permutation(part_keys[15], REQUESTS).astype(jnp.int32),
        "suffix_len": uneven(part_keys[16], REQUESTS, LIVE, SUF, 0).astype(jnp.int32),
    }


HIGH = lax.Precision.HIGHEST

def causal_conv(sequence, carried, weight):
    extended = jnp.concatenate([carried.astype(jnp.float32), sequence.astype(jnp.float32)], axis=1)
    summed = jnp.zeros(sequence.shape, jnp.float32)
    for tap_index in range(CONV):
        summed = summed + extended[:, tap_index:tap_index + SUF, :] * weight[tap_index].astype(jnp.float32)[None, None, :]
    return (summed, extended)

def ssd_spans(values, step_sizes, input_map, output_map, initial, decay_rate, skip_gain):
    log_steps = -step_sizes * decay_rate[None, None, :]
    cumulative = jnp.cumsum(log_steps, axis=1)
    by_head = jnp.transpose(cumulative, (0, 2, 1))
    spread = by_head[:, :, :, None] - by_head[:, :, None, :]
    length = values.shape[1]
    causal = jnp.arange(length)[:, None] >= jnp.arange(length)[None, :]
    decay_table = jnp.where(causal, jnp.exp(jnp.where(causal, spread, 0.0)), 0.0)
    scores = jnp.einsum('cthn,cshn->chts', output_map, input_map, precision=HIGH)
    mixing = scores * decay_table * jnp.transpose(step_sizes, (0, 2, 1))[:, :, None, :]
    inside = jnp.einsum('chts,cshp->cthp', mixing, values, precision=HIGH)
    tail_weights = jnp.exp(cumulative[:, -1:, :] - cumulative) * step_sizes
    local_states = jnp.einsum('cthp,cthn->chpn', values * tail_weights[..., None], input_map, precision=HIGH)
    span_decay = jnp.exp(cumulative[:, -1, :])

    def advance(carried, pair_in):
        advanced = pair_in[1][:, None, None] * carried + pair_in[0]
        return (advanced, carried)
    final_state, starts = lax.scan(advance, initial, (local_states, span_decay))
    across = jnp.einsum('cthn,chpn->cthp', output_map * jnp.exp(cumulative)[..., None], starts, precision=HIGH)
    output = inside + across + skip_gain[None, None, :, None] * values
    return (output, final_state)

def reference(ssm_input, gate_input, bc_input, dt_input, decay_rate, skip_gain, norm_gain, conv_x_weight, conv_bc_weight, out_weight, pool_states, pool_conv_x, pool_conv_bc, prefix_slot, prefix_spans, dest_slot, suffix_len):
    present = prefix_spans > 0
    start_states = jnp.where(present[:, None, None, None], pool_states[prefix_slot], jnp.zeros_like(pool_states[prefix_slot]))
    start_conv_x = jnp.where(present[:, None, None], pool_conv_x[prefix_slot], jnp.zeros_like(pool_conv_x[prefix_slot]))
    start_conv_bc = jnp.where(present[:, None, None], pool_conv_bc[prefix_slot], jnp.zeros_like(pool_conv_bc[prefix_slot]))
    positions = jnp.arange(SUF, dtype=jnp.int32)
    live_mask = (positions[None, :] < suffix_len[:, None]).astype(jnp.float32)
    conv_x, extended_x = causal_conv(ssm_input.reshape(REQUESTS, SUF, INNER), start_conv_x, conv_x_weight)
    values = jax.nn.silu(conv_x).astype(jnp.bfloat16)
    conv_bc, extended_bc = causal_conv(bc_input.reshape(REQUESTS, SUF, BCW), start_conv_bc, conv_bc_weight)
    maps = jax.nn.silu(conv_bc).astype(jnp.bfloat16)

    def tail_rows(extended, count):
        return lax.dynamic_slice_in_dim(extended, count, CONV - 1, 0)
    lengths = suffix_len.astype(jnp.int32)
    new_conv_x = jax.vmap(tail_rows)(extended_x, lengths)
    new_conv_bc = jax.vmap(tail_rows)(extended_bc, lengths)
    step_sizes = jax.nn.softplus(dt_input).reshape(REQUESTS, SUF, HEADS) * live_mask[:, :, None]
    maps_f = maps.astype(jnp.float32).reshape(REQUESTS, NCH, SPAN, 2, BCG, STATE)
    input_map = jnp.repeat(maps_f[:, :, :, 0], GHEADS, axis=3)
    output_map = jnp.repeat(maps_f[:, :, :, 1], GHEADS, axis=3)
    values_f = values.astype(jnp.float32).reshape(REQUESTS, NCH, SPAN, HEADS, HDIM)
    steps_c = step_sizes.reshape(REQUESTS, NCH, SPAN, HEADS)

    def one_request(inputs):
        return ssd_spans(inputs[0], inputs[1], inputs[2], inputs[3], inputs[4], decay_rate, skip_gain)
    outputs, finals = lax.map(one_request, (values_f, steps_c, input_map, output_map, start_states))
    gated = outputs.reshape(TOKENS, INNER) * jax.nn.silu(gate_input.astype(jnp.float32))
    mean_sq = lax.optimization_barrier(jnp.mean(gated * gated, axis=1))
    normed = (gated * lax.rsqrt(mean_sq + 1e-05)[:, None] * norm_gain[None, :]).astype(jnp.bfloat16)
    blocks_in = jnp.transpose(normed.reshape(TOKENS, N_TP, INNER // N_TP), (1, 0, 2))
    blocks_w = out_weight.reshape(N_TP, INNER // N_TP, D)

    def accumulate(carried, pair_in):
        partial_sum = jnp.dot(pair_in[0], pair_in[1], preferred_element_type=jnp.float32).astype(jnp.bfloat16)
        partial_sum = lax.optimization_barrier(partial_sum)
        return (carried + partial_sum.astype(jnp.float32), None)
    summed, unused = lax.scan(accumulate, jnp.zeros((TOKENS, D), jnp.float32), (blocks_in, blocks_w))
    mixed = (summed * live_mask.reshape(TOKENS)[:, None]).astype(jnp.bfloat16)
    ckpt_states = jnp.zeros_like(finals).at[dest_slot].set(finals)
    ckpt_conv_x = jnp.zeros_like(new_conv_x).at[dest_slot].set(new_conv_x).astype(jnp.bfloat16)
    ckpt_conv_bc = jnp.zeros_like(new_conv_bc).at[dest_slot].set(new_conv_bc).astype(jnp.bfloat16)
    return (mixed, ckpt_states, ckpt_conv_x, ckpt_conv_bc)
```

```python
import functools

import jax
import jax.numpy as jnp
from jax import lax
from jax.experimental import pallas as pl
from jax.experimental.pallas import tpu as pltpu
from jax.sharding import PartitionSpec as P

HDIM = 64
STATE = 128
GHEADS = 32
CONV = 4
SPAN = 128
SUF = 512
INNER = 8192
BCG = 4
BCW = 1024
NCH = 4
LANES = 128
WIDE = 512

F32 = jnp.float32
BF16 = jnp.bfloat16
HIGH = lax.Precision.HIGHEST


def silu(x):
    half = 0.5 * x
    return half + half * jnp.tanh(half)


def split_pair(x, heads):
    lane = lax.broadcasted_iota(jnp.int32, x.shape, 1)
    high = x.astype(BF16).astype(F32)
    rest = jnp.where(lane < 2 * heads, x - high, 0.0)
    return jnp.where(lane < heads, high, rest).astype(BF16)


def dot(a, b):
    return jnp.dot(a, b, preferred_element_type=F32)


def dot_t(a, b):
    return lax.dot_general(a, b, (((1,), (1,)), ((), ())), preferred_element_type=F32)


def conv_taps(before, x, weight):
    extended = jnp.concatenate([before, x], axis=0)
    total = extended[8:] * weight[CONV - 1 :]
    for k in range(CONV - 1):
        total += extended[5 + k : 5 + k + SPAN] * weight[k : k + 1]
    return total


def scan_kernel(
    heads,
    meta,
    x_ref,
    b_ref,
    c_ref,
    dt_ref,
    rate_ref,
    skip_ref,
    wx_ref,
    wb_ref,
    wc_ref,
    sx_ref,
    sb_ref,
    sc_ref,
    pick_ref,
    y_ref,
    final_ref,
    cmap_ref,
    reach_ref,
    total_ref,
    state,
    tail_x,
    tail_m,
    left,
    bmap_t,
    fac_a,
    fac_b,
    fac_row,
    base,
):
    block = pl.program_id(0)
    c = pl.program_id(1)

    @pl.when(block == 0)
    def _():
        maps = []
        for k, (ref, w, s) in enumerate(((b_ref, wb_ref, sb_ref), (c_ref, wc_ref, sc_ref))):
            before = jnp.where(c == 0, s[...], tail_m[k])
            x = ref[...].astype(F32)
            maps.append(silu(conv_taps(before, x, w[...].astype(F32))).astype(BF16))
            tail_m[k] = x[SPAN - 8 :]
        bmap, cmap = maps
        row = lax.broadcasted_iota(jnp.int32, (SPAN, SPAN), 0)
        col = lax.broadcasted_iota(jnp.int32, (SPAN, SPAN), 1)
        scores = jnp.where(row >= col, dot_t(cmap, bmap), 0.0).astype(BF16)
        left[c, :, :SPAN] = scores
        left[c, :, SPAN:] = cmap
        cmap_ref[...] = cmap
        bmap_t[c] = jnp.transpose(bmap.astype(F32)).astype(BF16)

        @pl.when(c == 0)
        def _():
            base[...] = jnp.zeros_like(base)

        logit = dt_ref[...]
        live = (row + c * SPAN < meta[1]).astype(F32)
        step = (jnp.maximum(logit, 0.0) + jnp.log1p(jnp.exp(-jnp.abs(logit)))) * live
        cum = jnp.dot(
            (row >= col).astype(F32),
            -step * rate_ref[...],
            precision=HIGH,
            preferred_element_type=F32,
        )
        last = cum[SPAN - 1 :]
        mid = 0.5 * last
        fac_a[c] = split_pair(jnp.exp(cum - mid), heads)
        fac_b[c] = split_pair(jnp.exp(mid - cum) * step, heads)
        before = base[0:1]
        reach_ref[...] = split_pair(jnp.exp(before + cum), heads)
        which = lax.broadcasted_iota(jnp.int32, (16, LANES), 0)
        fac_row[c] = split_pair(
            jnp.where(which == 0, jnp.exp(mid), jnp.exp(last - mid)) + jnp.zeros((16, LANES), F32),
            heads,
        )
        base[...] = base[...] + last
        total_ref[...] = jnp.exp(base[...])

    @pl.when(c == 0)
    def _():
        state[...] = jnp.zeros_like(state)
        tail_x[...] = sx_ref[...]

    pick = pick_ref[...]
    x = x_ref[...].astype(F32)
    conv = conv_taps(tail_x[...], x, wx_ref[...].astype(F32))
    tail_x[...] = x[SPAN - 8 :]
    values = silu(conv).astype(BF16).astype(F32)
    scaled = (values * dot(fac_b[c], pick)).astype(BF16)
    rows = dot(fac_row[c], pick)
    held = state[...] * rows[0:1]
    right = jnp.concatenate([scaled, held.astype(BF16)], axis=0)
    y_ref[...] = dot(left[c], right) * dot(fac_a[c], pick) + skip_ref[...] * values
    state[...] = (held + dot(bmap_t[c], scaled)) * rows[1:2]

    @pl.when(c == NCH - 1)
    def _():
        final_ref[...] = jnp.transpose(state[...])


def run_scan(meta, x, bc, dt, rate, skip, wx, wbc, sx, sbc, pick, heads):
    inner = x.shape[1]
    blocks = inner // WIDE
    once = lambda b, c: jnp.where(b == 0, c, NCH - 1)
    in_specs = [
        pl.BlockSpec((SPAN, WIDE), lambda b, c, m: (c, b)),
        pl.BlockSpec((SPAN, LANES), lambda b, c, m: (once(b, c), m[0])),
        pl.BlockSpec((SPAN, LANES), lambda b, c, m: (once(b, c), m[0] + BCG)),
        pl.BlockSpec((SPAN, LANES), lambda b, c, m: (once(b, c), 0)),
        pl.BlockSpec((1, LANES), lambda b, c, m: (0, 0)),
        pl.BlockSpec((1, WIDE), lambda b, c, m: (0, b)),
        pl.BlockSpec((CONV, WIDE), lambda b, c, m: (0, b)),
        pl.BlockSpec((CONV, LANES), lambda b, c, m: (0, m[0])),
        pl.BlockSpec((CONV, LANES), lambda b, c, m: (0, m[0] + BCG)),
        pl.BlockSpec((8, WIDE), lambda b, c, m: (0, b)),
        pl.BlockSpec((8, LANES), lambda b, c, m: (0, m[0])),
        pl.BlockSpec((8, LANES), lambda b, c, m: (0, m[0] + BCG)),
        pl.BlockSpec((LANES, WIDE), lambda b, c, m: (0, b)),
    ]
    out_specs = [
        pl.BlockSpec((SPAN, WIDE), lambda b, c, m: (c, b)),
        pl.BlockSpec((WIDE, STATE), lambda b, c, m: (b, 0)),
        pl.BlockSpec((SPAN, LANES), lambda b, c, m: (once(b, c), 0)),
        pl.BlockSpec((SPAN, LANES), lambda b, c, m: (once(b, c), 0)),
        pl.BlockSpec((8, LANES), lambda b, c, m: (0, 0)),
    ]
    return pl.pallas_call(
        functools.partial(scan_kernel, heads),
        grid_spec=pltpu.PrefetchScalarGridSpec(
            num_scalar_prefetch=1,
            grid=(blocks, NCH),
            in_specs=in_specs,
            out_specs=out_specs,
            scratch_shapes=[
                pltpu.VMEM((STATE, WIDE), F32),
                pltpu.VMEM((8, WIDE), F32),
                pltpu.VMEM((2, 8, LANES), F32),
                pltpu.VMEM((NCH, SPAN, 2 * SPAN), BF16),
                pltpu.VMEM((NCH, STATE, SPAN), BF16),
                pltpu.VMEM((NCH, SPAN, LANES), BF16),
                pltpu.VMEM((NCH, SPAN, LANES), BF16),
                pltpu.VMEM((NCH, 16, LANES), BF16),
                pltpu.VMEM((8, LANES), F32),
            ],
        ),
        out_shape=[
            jax.ShapeDtypeStruct((SUF, inner), F32),
            jax.ShapeDtypeStruct((inner, STATE), F32),
            jax.ShapeDtypeStruct((SUF, LANES), BF16),
            jax.ShapeDtypeStruct((SUF, LANES), BF16),
            jax.ShapeDtypeStruct((8, LANES), F32),
        ],
        compiler_params=pltpu.CompilerParams(
            dimension_semantics=("arbitrary", "arbitrary"), vmem_limit_bytes=24 * 2**20
        ),
        cost_estimate=pl.CostEstimate(
            flops=8 * 10**9, bytes_accessed=12 * 2**20, transcendentals=SUF * inner
        ),
        name="local_scan",
    )(meta, x, bc, bc, dt, rate, skip, wx, wbc, wbc, sx, sbc, sbc, pick)


def project_kernel(
    y_ref, gate_ref, cmap_ref, reach_ref, start_ref, gain_ref, pick_ref, w_ref, out_ref, sq_ref, held
):
    @pl.when(pl.program_id(0) == 0)
    def _():
        inner = y_ref.shape[1]
        squares = jnp.zeros((SPAN, LANES), F32)
        for i in range(inner // WIDE):
            at = pl.ds(i * WIDE, WIDE)
            carried = dot_t(cmap_ref[...], start_ref[at, :])
            y = y_ref[:, at] + dot(reach_ref[...], pick_ref[:, at]) * carried
            gated = y * silu(gate_ref[:, at].astype(F32))
            held[:, at] = (gated * gain_ref[:, at]).astype(BF16)
            gated = gated * gated
            for j in range(WIDE // LANES):
                squares += gated[:, j * LANES : (j + 1) * LANES]
        sq_ref[...] = lax.dot_general(
            jnp.ones((8, LANES), F32),
            squares,
            (((1,), (1,)), ((), ())),
            precision=HIGH,
            preferred_element_type=F32,
        )

    out_ref[0] = dot(held[...], w_ref[...]).astype(BF16)


def run_project(piece, y, gate, cmap, reach, start, gain, pick, weight, shares):
    inner, width = weight.shape
    share = width // shares
    rows = lambda n: (piece, 0)
    whole = lambda n: (0, 0)
    return pl.pallas_call(
        project_kernel,
        grid=(shares,),
        in_specs=[
            pl.BlockSpec((SPAN, inner), rows),
            pl.BlockSpec((SPAN, inner), rows),
            pl.BlockSpec((SPAN, LANES), rows),
            pl.BlockSpec((SPAN, LANES), rows),
            pl.BlockSpec((inner, STATE), whole),
            pl.BlockSpec((1, inner), whole),
            pl.BlockSpec((LANES, inner), whole),
            pl.BlockSpec((inner, share), lambda n: (0, n)),
        ],
        out_specs=[
            pl.BlockSpec((1, SPAN, share), lambda n: (n, 0, 0)),
            pl.BlockSpec((8, LANES), whole),
        ],
        out_shape=[
            jax.ShapeDtypeStruct((shares, SPAN, share), BF16),
            jax.ShapeDtypeStruct((8, LANES), F32),
        ],
        scratch_shapes=[pltpu.VMEM((SPAN, inner), BF16)],
        compiler_params=pltpu.CompilerParams(
            dimension_semantics=("arbitrary",), vmem_limit_bytes=32 * 2**20
        ),
        cost_estimate=pl.CostEstimate(
            flops=2 * SPAN * inner * width,
            bytes_accessed=2 * inner * width + 3 * 2**20,
            transcendentals=SPAN * inner,
        ),
        name="project",
    )(y, gate, cmap, reach, start, gain, pick, weight)


def shifted(x, axis, size, by):
    return lax.ppermute(x, axis, [(i, (i + by) % size) for i in range(size)])


def swap_core(x, size):
    return lax.ppermute(x, "req", [(i, i ^ 1) for i in range(size)])


def per_device(
    ssm_input,
    gate_input,
    bc_input,
    dt_input,
    decay_rate,
    skip_gain,
    norm_gain,
    conv_x_weight,
    conv_bc_weight,
    out_weight,
    pool_states,
    pool_conv_x,
    pool_conv_bc,
    prefix_slot,
    prefix_spans,
    dest_slot,
    suffix_len,
):
    num_req = lax.axis_size("req")
    num_tp = lax.axis_size("tp")
    me = lax.axis_index("req")
    z = lax.axis_index("tp")
    mate = me ^ 1
    heads = dt_input.shape[1]
    inner = ssm_input.shape[1]
    slots = pool_states.shape[0]
    copies = LANES // heads

    my_len = suffix_len[me]
    my_slot = prefix_slot[me]
    my_present = prefix_spans[me] > 0

    pool_conv = jnp.concatenate([pool_conv_x, pool_conv_bc], axis=2)

    def conv_for(request):
        return lax.dynamic_index_in_dim(
            pool_conv, jnp.clip(prefix_slot[request] - slots * me, 0, slots - 1), 0, False
        )

    start_conv = conv_for(me)
    for by in range(1, num_req):
        got = shifted(conv_for((me + by) % num_req), "req", num_req, by)
        start_conv = jnp.where(my_slot // slots == (me - by) % num_req, got, start_conv)
    start_conv = jnp.where(my_present, start_conv, jnp.zeros_like(start_conv))

    pool_flat = pool_states.astype(BF16).reshape(slots, inner, STATE)
    pool_mate = swap_core(pool_flat, num_req)

    def state_for(request):
        slot = prefix_slot[request]
        mine = lax.dynamic_index_in_dim(
            pool_flat, jnp.clip(slot - slots * me, 0, slots - 1), 0, False
        )
        other = lax.dynamic_index_in_dim(
            pool_mate, jnp.clip(slot - slots * mate, 0, slots - 1), 0, False
        )
        return jnp.where(slot // slots == me, mine, other)

    start = state_for(me)
    for by in range(2, num_req, 2):
        got = shifted(state_for((me + by) % num_req), "req", num_req, by)
        start = jnp.where(my_slot // (2 * slots) == ((me - by) % num_req) // 2, got, start)
    start = jnp.where(my_present, start, jnp.zeros_like(start))

    before = jnp.pad(start_conv.astype(F32), ((8 - (CONV - 1), 0), (0, 0)))
    lane_head = jnp.arange(LANES)[:, None]
    pick = (
        (lane_head % heads == (jnp.arange(inner) // HDIM)[None, :]) & (lane_head < 2 * heads)
    ).astype(BF16)
    meta = jnp.stack([(z * heads) // GHEADS, my_len]).astype(jnp.int32)
    y_local, local_final, cmap, reach, total = run_scan(
        meta,
        ssm_input,
        bc_input,
        jnp.tile(dt_input, (1, copies)),
        jnp.tile(decay_rate, copies)[None, :],
        jnp.repeat(skip_gain, HDIM)[None, :],
        conv_x_weight,
        conv_bc_weight,
        before[:, :inner],
        before[:, inner:],
        pick,
        heads,
    )

    gain = norm_gain[None, :]
    to_right = [(i, i + 1) for i in range(num_tp - 1)]
    to_left = [(i + 1, i) for i in range(num_tp - 1)]
    squares, summed = [], []
    for piece in range(NCH):
        part, square = run_project(
            piece, y_local, gate_input, cmap, reach, start, gain, pick, out_weight, num_tp
        )
        squares.append(square[0])

        def share(at):
            return lax.dynamic_index_in_dim(part, jnp.clip(at, 0, num_tp - 1), 0, False)

        right = left = None
        for s in range(num_tp - 1):
            go_right = share(num_tp - 1 - s + z)
            go_left = share(s - (num_tp - 1) + z)
            if s:
                go_right = (go_right.astype(F32) + right.astype(F32)).astype(BF16)
                go_left = (go_left.astype(F32) + left.astype(F32)).astype(BF16)
            right = lax.ppermute(go_right, "tp", to_right[: s + 1])
            left = lax.ppermute(go_left, "tp", to_left[num_tp - 2 - s :])
        summed.append(share(z).astype(F32) + right.astype(F32) + left.astype(F32))

    square = jnp.concatenate(squares)
    square_total = square
    for by in range(1, num_tp):
        square_total = square_total + shifted(square, "tp", num_tp, by)
    scale = lax.rsqrt(square_total / INNER + 1e-05)
    scale = jnp.where(jnp.arange(SUF) < my_len, scale, 0.0)
    mixed = (jnp.concatenate(summed, axis=0) * scale[:, None]).astype(BF16)

    decay = jnp.repeat(total[0, :heads], HDIM)[:, None]
    final = (local_final + decay * start.astype(F32)).astype(BF16)
    source = jnp.argmax(dest_slot[None, :] == jnp.arange(num_req)[:, None], axis=1)
    for_me = for_mate = final
    for by in range(2, num_req, 2):
        got = shifted(final, "req", num_req, by)
        origin = (me - by) % num_req
        for_me = jnp.where(source[me] == origin, got, for_me)
        for_mate = jnp.where(source[mate] == origin, got, for_mate)
    crossed = swap_core(for_mate, num_req)
    ckpt = jnp.where(source[me] % 2 == me % 2, for_me, crossed)
    ckpt_states = ckpt.astype(F32).reshape((1, heads, HDIM, STATE))

    extended_x = jnp.concatenate([start_conv[:, :inner], ssm_input], axis=0)
    extended_bc = jnp.concatenate([start_conv[:, inner:], bc_input], axis=0)
    tail = jnp.concatenate(
        [
            lax.dynamic_slice_in_dim(extended_x, my_len, CONV - 1, 0),
            lax.dynamic_slice_in_dim(extended_bc, my_len, CONV - 1, 0),
        ],
        axis=1,
    )
    landed = tail
    for by in range(1, num_req):
        got = shifted(tail, "req", num_req, by)
        landed = jnp.where(source[me] == (me - by) % num_req, got, landed)
    return (mixed, ckpt_states, landed[None, :, :inner], landed[None, :, inner:])


def solution(mesh):
    return jax.shard_map(
        per_device,
        mesh=mesh,
        in_specs=(
            P(("groups", "req"), "tp"),
            P(("groups", "req"), "tp"),
            P(("groups", "req"), None),
            P(("groups", "req"), "tp"),
            P("tp"),
            P("tp"),
            P("tp"),
            P(None, "tp"),
            P(),
            P("tp", None),
            P(("groups", "req"), "tp", None, None),
            P(("groups", "req"), None, "tp"),
            P(("groups", "req"), None, None),
            P("groups"),
            P("groups"),
            P("groups"),
            P("groups"),
        ),
        out_specs=(
            P(("groups", "req"), "tp"),
            P(("groups", "req"), "tp", None, None),
            P(("groups", "req"), None, "tp"),
            P(("groups", "req"), None, None),
        ),
        check_vma=False,
    )
```

```python
import functools

import jax
import jax.numpy as jnp
from jax import lax
from jax.experimental import pallas as pl
from jax.experimental.pallas import tpu as pltpu
from jax.sharding import PartitionSpec as P

HDIM = 64
STATE = 128
GHEADS = 32
CONV = 4
SPAN = 128
SUF = 512
INNER = 8192
BCG = 4
BCW = 1024
NCH = 4
LANES = 128
WIDE = 512

F32 = jnp.float32
BF16 = jnp.bfloat16
HIGH = lax.Precision.HIGHEST


def silu(x):
    half = 0.5 * x
    return half + half * jnp.tanh(half)


def split_pair(x, heads):
    lane = lax.broadcasted_iota(jnp.int32, x.shape, 1)
    high = x.astype(BF16).astype(F32)
    rest = jnp.where(lane < 2 * heads, x - high, 0.0)
    return jnp.where(lane < heads, high, rest).astype(BF16)


def dot(a, b):
    return jnp.dot(a, b, preferred_element_type=F32)


def dot_t(a, b):
    return lax.dot_general(a, b, (((1,), (1,)), ((), ())), preferred_element_type=F32)


def conv_taps(before, x, weight):
    extended = jnp.concatenate([before, x], axis=0)
    total = extended[8:] * weight[CONV - 1 :]
    for k in range(CONV - 1):
        total += extended[5 + k : 5 + k + SPAN] * weight[k : k + 1]
    return total


def pack_kernel(reqs, meta, pool_ref, px_ref, pb_ref, states_ref, conv_ref):
    slots = pool_ref.shape[0]
    inner = px_ref.shape[2]
    me = meta[0]
    for s in range(slots):
        states_ref[s] = pool_ref[s].astype(BF16)
    for by in range(reqs):
        at = jnp.clip(meta[2 + (me + by) % reqs] - slots * me, 0, slots - 1)
        conv_ref[by, :, :inner] = px_ref[at]
        conv_ref[by, :, inner:] = pb_ref[at]


def run_pack(meta, pool, px, pb, reqs):
    slots, inner, _ = pool.shape
    return pl.pallas_call(
        functools.partial(pack_kernel, reqs),
        grid_spec=pltpu.PrefetchScalarGridSpec(
            num_scalar_prefetch=1,
            grid=(1,),
            in_specs=[
                pl.BlockSpec(pool.shape, lambda i, m: (0, 0, 0)),
                pl.BlockSpec(px.shape, lambda i, m: (0, 0, 0)),
                pl.BlockSpec(pb.shape, lambda i, m: (0, 0, 0)),
            ],
            out_specs=[
                pl.BlockSpec(pool.shape, lambda i, m: (0, 0, 0)),
                pl.BlockSpec((reqs, CONV - 1, inner + BCW), lambda i, m: (0, 0, 0)),
            ],
        ),
        out_shape=[
            jax.ShapeDtypeStruct(pool.shape, BF16),
            jax.ShapeDtypeStruct((reqs, CONV - 1, inner + BCW), BF16),
        ],
        compiler_params=pltpu.CompilerParams(vmem_limit_bytes=16 * 2**20),
        cost_estimate=pl.CostEstimate(flops=10**6, bytes_accessed=3 * 2**20, transcendentals=0),
        name="pack",
    )(meta, pool, px, pb)


def choose_kernel(reqs, slots, meta, mine_ref, mate_ref, out_ref):
    slot = meta[2 + (meta[0] + 2 + 2 * pl.program_id(0)) % reqs]
    out_ref[...] = jnp.where(slot // slots == meta[0], mine_ref[...], mate_ref[...])


def run_choose(meta, mine, mate, reqs):
    slots, inner, _ = mine.shape
    shape = (1, inner, STATE)

    def held(meta, by, owner):
        return jnp.clip(meta[2 + (meta[0] + 2 + 2 * by) % reqs] - slots * owner, 0, slots - 1)

    return pl.pallas_call(
        functools.partial(choose_kernel, reqs, slots),
        grid_spec=pltpu.PrefetchScalarGridSpec(
            num_scalar_prefetch=1,
            grid=(reqs // 2 - 1,),
            in_specs=[
                pl.BlockSpec(shape, lambda i, m: (held(m, i, m[0]), 0, 0)),
                pl.BlockSpec(shape, lambda i, m: (held(m, i, m[0] ^ 1), 0, 0)),
            ],
            out_specs=pl.BlockSpec(shape, lambda i, m: (i, 0, 0)),
        ),
        out_shape=jax.ShapeDtypeStruct((reqs // 2 - 1, inner, STATE), BF16),
        compiler_params=pltpu.CompilerParams(vmem_limit_bytes=16 * 2**20),
        cost_estimate=pl.CostEstimate(flops=10**6, bytes_accessed=2 * 2**20, transcendentals=0),
        name="choose",
    )(meta, mine, mate)


def scan_kernel(
    heads,
    slots,
    reqs,
    meta,
    *refs,
):
    scan_body(heads, slots, reqs, meta, refs[:reqs], *refs[reqs:])


def scan_body(
    heads,
    slots,
    reqs,
    meta,
    conv_refs,
    x_ref,
    b_ref,
    c_ref,
    dt_ref,
    rate_ref,
    skip_ref,
    wx_ref,
    wb_ref,
    wc_ref,
    pick_ref,
    y_ref,
    final_ref,
    cmap_ref,
    reach_ref,
    total_ref,
    conv_ref,
    start,
    state,
    tail_x,
    tail_m,
    left,
    bmap_t,
    fac_a,
    fac_b,
    fac_row,
    base,
):
    block = pl.program_id(0)
    c = pl.program_id(1)
    me = meta[0]
    slot = meta[2 + me]
    inner = conv_ref.shape[1] - BCW
    group = (meta[1] * heads) // GHEADS

    @pl.when((block == 0) & (c == 0))
    def _():
        away = (me - slot // slots + reqs) % reqs
        taken = conv_refs[0][0].astype(F32)
        for by in range(1, reqs):
            taken = jnp.where(away == by, conv_refs[by][...].astype(F32), taken)
        taken = jnp.where(meta[2 + reqs + me] > 0, taken, 0.0)
        start[...] = jnp.concatenate(
            [jnp.zeros((8 - (CONV - 1), inner + BCW), F32), taken], axis=0
        )
        conv_ref[...] = taken.astype(BF16)

    @pl.when(block == 0)
    def _():
        maps = []
        for k, (ref, w) in enumerate(((b_ref, wb_ref), (c_ref, wc_ref))):
            at = pl.multiple_of(inner + (group + k * BCG) * LANES, LANES)
            before = jnp.where(c == 0, start[:, pl.ds(at, LANES)], tail_m[k])
            x = ref[...].astype(F32)
            maps.append(silu(conv_taps(before, x, w[...].astype(F32))).astype(BF16))
            tail_m[k] = x[SPAN - 8 :]
        bmap, cmap = maps
        row = lax.broadcasted_iota(jnp.int32, (SPAN, SPAN), 0)
        col = lax.broadcasted_iota(jnp.int32, (SPAN, SPAN), 1)
        scores = jnp.where(row >= col, dot_t(cmap, bmap), 0.0).astype(BF16)
        left[c, :, :SPAN] = scores
        left[c, :, SPAN:] = cmap
        cmap_ref[...] = cmap
        bmap_t[c] = jnp.transpose(bmap.astype(F32)).astype(BF16)

        @pl.when(c == 0)
        def _():
            base[...] = jnp.zeros_like(base)

        logit = dt_ref[...]
        live = (row + c * SPAN < meta[2 + 3 * reqs + me]).astype(F32)
        step = (jnp.maximum(logit, 0.0) + jnp.log1p(jnp.exp(-jnp.abs(logit)))) * live
        cum = jnp.dot(
            (row >= col).astype(F32),
            -step * rate_ref[...],
            precision=HIGH,
            preferred_element_type=F32,
        )
        last = cum[SPAN - 1 :]
        mid = 0.5 * last
        fac_a[c] = split_pair(jnp.exp(cum - mid), heads)
        fac_b[c] = split_pair(jnp.exp(mid - cum) * step, heads)
        before = base[0:1]
        reach_ref[...] = split_pair(jnp.exp(before + cum), heads)
        which = lax.broadcasted_iota(jnp.int32, (16, LANES), 0)
        fac_row[c] = split_pair(
            jnp.where(which == 0, jnp.exp(mid), jnp.exp(last - mid)) + jnp.zeros((16, LANES), F32),
            heads,
        )
        base[...] = base[...] + last
        total_ref[...] = jnp.exp(base[...])

    @pl.when(c == 0)
    def _():
        state[...] = jnp.zeros_like(state)
        tail_x[...] = start[:, pl.ds(pl.multiple_of(block * WIDE, WIDE), WIDE)]

    pick = pick_ref[...]
    x = x_ref[...].astype(F32)
    conv = conv_taps(tail_x[...], x, wx_ref[...].astype(F32))
    tail_x[...] = x[SPAN - 8 :]
    values = silu(conv).astype(BF16).astype(F32)
    scaled = (values * dot(fac_b[c], pick)).astype(BF16)
    rows = dot(fac_row[c], pick)
    held = state[...] * rows[0:1]
    right = jnp.concatenate([scaled, held.astype(BF16)], axis=0)
    y_ref[...] = dot(left[c], right) * dot(fac_a[c], pick) + skip_ref[...] * values
    state[...] = (held + dot(bmap_t[c], scaled)) * rows[1:2]

    @pl.when(c == NCH - 1)
    def _():
        final_ref[...] = jnp.transpose(state[...])


def run_scan(meta, conv, x, bc, dt, rate, skip, wx, wbc, pick, heads, slots):
    inner = x.shape[1]
    blocks = inner // WIDE
    reqs = len(conv)
    once = lambda b, c: jnp.where(b == 0, c, NCH - 1)
    group = lambda m: (m[1] * heads) // GHEADS
    in_specs = [pl.BlockSpec((1, CONV - 1, inner + BCW), lambda b, c, m: (0, 0, 0))]
    in_specs += [pl.BlockSpec((CONV - 1, inner + BCW), lambda b, c, m: (0, 0))] * (reqs - 1)
    in_specs += [
        pl.BlockSpec((SPAN, WIDE), lambda b, c, m: (c, b)),
        pl.BlockSpec((SPAN, LANES), lambda b, c, m: (once(b, c), group(m))),
        pl.BlockSpec((SPAN, LANES), lambda b, c, m: (once(b, c), group(m) + BCG)),
        pl.BlockSpec((SPAN, LANES), lambda b, c, m: (once(b, c), 0)),
        pl.BlockSpec((1, LANES), lambda b, c, m: (0, 0)),
        pl.BlockSpec((1, WIDE), lambda b, c, m: (0, b)),
        pl.BlockSpec((CONV, WIDE), lambda b, c, m: (0, b)),
        pl.BlockSpec((CONV, LANES), lambda b, c, m: (0, group(m))),
        pl.BlockSpec((CONV, LANES), lambda b, c, m: (0, group(m) + BCG)),
        pl.BlockSpec((LANES, WIDE), lambda b, c, m: (0, b)),
    ]
    out_specs = [
        pl.BlockSpec((SPAN, WIDE), lambda b, c, m: (c, b)),
        pl.BlockSpec((WIDE, STATE), lambda b, c, m: (b, 0)),
        pl.BlockSpec((SPAN, LANES), lambda b, c, m: (once(b, c), 0)),
        pl.BlockSpec((SPAN, LANES), lambda b, c, m: (once(b, c), 0)),
        pl.BlockSpec((8, LANES), lambda b, c, m: (0, 0)),
        pl.BlockSpec((CONV - 1, inner + BCW), lambda b, c, m: (0, 0)),
    ]
    return pl.pallas_call(
        functools.partial(scan_kernel, heads, slots, reqs),
        grid_spec=pltpu.PrefetchScalarGridSpec(
            num_scalar_prefetch=1,
            grid=(blocks, NCH),
            in_specs=in_specs,
            out_specs=out_specs,
            scratch_shapes=[
                pltpu.VMEM((8, inner + BCW), F32),
                pltpu.VMEM((STATE, WIDE), F32),
                pltpu.VMEM((8, WIDE), F32),
                pltpu.VMEM((2, 8, LANES), F32),
                pltpu.VMEM((NCH, SPAN, 2 * SPAN), BF16),
                pltpu.VMEM((NCH, STATE, SPAN), BF16),
                pltpu.VMEM((NCH, SPAN, LANES), BF16),
                pltpu.VMEM((NCH, SPAN, LANES), BF16),
                pltpu.VMEM((NCH, 16, LANES), BF16),
                pltpu.VMEM((8, LANES), F32),
            ],
        ),
        out_shape=[
            jax.ShapeDtypeStruct((SUF, inner), F32),
            jax.ShapeDtypeStruct((inner, STATE), F32),
            jax.ShapeDtypeStruct((SUF, LANES), BF16),
            jax.ShapeDtypeStruct((SUF, LANES), BF16),
            jax.ShapeDtypeStruct((8, LANES), F32),
            jax.ShapeDtypeStruct((CONV - 1, inner + BCW), BF16),
        ],
        compiler_params=pltpu.CompilerParams(
            dimension_semantics=("arbitrary", "arbitrary"), vmem_limit_bytes=24 * 2**20
        ),
        cost_estimate=pl.CostEstimate(
            flops=8 * 10**9, bytes_accessed=12 * 2**20, transcendentals=SUF * inner
        ),
        name="local_scan",
    )(meta, *conv, x, bc, bc, dt, rate, skip, wx, wbc, wbc, pick)


def project_kernel(reqs, slots, meta, *refs):
    others = reqs // 2 - 1
    mine_ref, mate_ref = refs[:2]
    got_refs = refs[2 : 2 + others]
    (
        y_ref,
        gate_ref,
        cmap_ref,
        reach_ref,
        gain_ref,
        pick_ref,
        w_ref,
        out_ref,
        sq_ref,
        start_ref,
        held,
    ) = refs[2 + others :]
    step = pl.program_id(0)
    me = meta[0]
    inner = y_ref.shape[1]

    @pl.when(step == 0)
    def _():
        owner = meta[2 + me] // slots
        away = (me // 2 - owner // 2 + reqs // 2) % (reqs // 2)
        taken = jnp.where(owner == me, mine_ref[0], mate_ref[0])
        for k in range(others):
            taken = jnp.where(away == k + 1, got_refs[k][0], taken)
        start_ref[...] = jnp.where(meta[2 + reqs + me] > 0, taken, jnp.zeros_like(taken))

    @pl.when(step < NCH)
    def _():
        squares = jnp.zeros((SPAN, LANES), F32)
        rows = pl.ds(pl.multiple_of(step * SPAN, SPAN), SPAN)
        for i in range(inner // WIDE):
            at = pl.ds(i * WIDE, WIDE)
            carried = dot_t(cmap_ref[...], start_ref[at, :])
            y = y_ref[:, at] + dot(reach_ref[...], pick_ref[:, at]) * carried
            gated = y * silu(gate_ref[:, at].astype(F32))
            held[rows, at] = (gated * gain_ref[:, at]).astype(BF16)
            gated = gated * gated
            for j in range(WIDE // LANES):
                squares += gated[:, j * LANES : (j + 1) * LANES]
        sq_ref[...] = lax.dot_general(
            jnp.ones((8, LANES), F32),
            squares,
            (((1,), (1,)), ((), ())),
            precision=HIGH,
            preferred_element_type=F32,
        )

    @pl.when(step >= NCH)
    def _():
        out_ref[0] = dot(held[...], w_ref[...]).astype(BF16)


def run_project(meta, mine, mate, got, y, gate, cmap, reach, gain, pick, weight, shares):
    slots = mine.shape[0]
    reqs = 2 * len(got) + 2
    inner, width = weight.shape
    share = width // shares
    tile = min(share, WIDE)
    per = share // tile
    rows = lambda n, m: (jnp.minimum(n, NCH - 1), 0)
    whole = lambda n, m: (0, 0)
    column = lambda n: jnp.maximum(n - NCH, 0)
    state = (1, inner, STATE)

    def held(owner, m):
        return jnp.clip(m[2 + m[0]] - slots * owner, 0, slots - 1)

    return pl.pallas_call(
        functools.partial(project_kernel, reqs, slots),
        grid_spec=pltpu.PrefetchScalarGridSpec(
            num_scalar_prefetch=1,
            grid=(NCH + width // tile,),
            in_specs=[
                pl.BlockSpec(state, lambda n, m: (held(m[0], m), 0, 0)),
                pl.BlockSpec(state, lambda n, m: (held(m[0] ^ 1, m), 0, 0)),
            ]
            + [pl.BlockSpec(state, lambda n, m: (0, 0, 0))] * len(got)
            + [
                pl.BlockSpec((SPAN, inner), rows),
                pl.BlockSpec((SPAN, inner), rows),
                pl.BlockSpec((SPAN, LANES), rows),
                pl.BlockSpec((SPAN, LANES), rows),
                pl.BlockSpec((1, inner), whole),
                pl.BlockSpec((LANES, inner), whole),
                pl.BlockSpec((inner, tile), lambda n, m: (0, column(n))),
            ],
            out_specs=[
                pl.BlockSpec((1, SUF, tile), lambda n, m: (column(n) // per, 0, column(n) % per)),
                pl.BlockSpec((8, LANES), lambda n, m: (0, jnp.minimum(n, NCH - 1))),
                pl.BlockSpec((inner, STATE), whole),
            ],
            scratch_shapes=[pltpu.VMEM((SUF, inner), BF16)],
        ),
        out_shape=[
            jax.ShapeDtypeStruct((shares, SUF, share), BF16),
            jax.ShapeDtypeStruct((8, SUF), F32),
            jax.ShapeDtypeStruct((inner, STATE), BF16),
        ],
        compiler_params=pltpu.CompilerParams(
            dimension_semantics=("arbitrary",), vmem_limit_bytes=40 * 2**20
        ),
        cost_estimate=pl.CostEstimate(
            flops=2 * SUF * inner * width,
            bytes_accessed=2 * inner * width + 10 * 2**20,
            transcendentals=SUF * inner,
        ),
        name="project",
    )(meta, mine, mate, *got, y, gate, cmap, reach, gain, pick, weight)


def shifted(x, axis, size, by):
    return lax.ppermute(x, axis, [(i, (i + by) % size) for i in range(size)])


def swap_core(x, size):
    return lax.ppermute(x, "req", [(i, i ^ 1) for i in range(size)])


def per_device(
    ssm_input,
    gate_input,
    bc_input,
    dt_input,
    decay_rate,
    skip_gain,
    norm_gain,
    conv_x_weight,
    conv_bc_weight,
    out_weight,
    pool_states,
    pool_conv_x,
    pool_conv_bc,
    prefix_slot,
    prefix_spans,
    dest_slot,
    suffix_len,
):
    num_req = lax.axis_size("req")
    num_tp = lax.axis_size("tp")
    me = lax.axis_index("req")
    z = lax.axis_index("tp")
    mate = me ^ 1
    heads = dt_input.shape[1]
    inner = ssm_input.shape[1]
    slots = pool_states.shape[0]
    copies = LANES // heads
    meta = jnp.concatenate(
        [jnp.stack([me, z]), prefix_slot, prefix_spans, dest_slot, suffix_len]
    ).astype(jnp.int32)

    mine, conv = run_pack(
        meta, pool_states.reshape(slots, inner, STATE), pool_conv_x, pool_conv_bc, num_req
    )
    other = swap_core(mine, num_req)
    convs = [conv] + [shifted(conv[by], "req", num_req, by) for by in range(1, num_req)]
    chosen = run_choose(meta, mine, other, num_req)
    got = [
        shifted(chosen[k : k + 1], "req", num_req, 2 * k + 2) for k in range(num_req // 2 - 1)
    ]

    lane_head = jnp.arange(LANES)[:, None]
    pick = (
        (lane_head % heads == (jnp.arange(inner) // HDIM)[None, :]) & (lane_head < 2 * heads)
    ).astype(BF16)
    y_local, local_final, cmap, reach, total, start_conv = run_scan(
        meta,
        convs,
        ssm_input,
        bc_input,
        jnp.tile(dt_input, (1, copies)),
        jnp.tile(decay_rate, copies)[None, :],
        jnp.repeat(skip_gain, HDIM)[None, :],
        conv_x_weight,
        conv_bc_weight,
        pick,
        heads,
        slots,
    )
    part, square, start = run_project(
        meta,
        mine,
        other,
        got,
        y_local,
        gate_input,
        cmap,
        reach,
        norm_gain[None, :],
        pick,
        out_weight,
        num_tp,
    )
    summed = lax.psum_scatter(part, "tp", scatter_dimension=0, tiled=True)[0].astype(F32)

    my_len = suffix_len[me]
    square = square[0]
    square_total = square
    for by in range(1, num_tp):
        square_total = square_total + shifted(square, "tp", num_tp, by)
    scale = lax.rsqrt(square_total / INNER + 1e-05)
    scale = jnp.where(jnp.arange(SUF) < my_len, scale, 0.0)
    mixed = (summed * scale[:, None]).astype(BF16)

    decay = jnp.repeat(total[0, :heads], HDIM)[:, None]
    final = (local_final + decay * start.astype(F32)).astype(BF16)
    source = jnp.argmax(dest_slot[None, :] == jnp.arange(num_req)[:, None], axis=1)
    for_me = for_mate = final
    for by in range(2, num_req, 2):
        got = shifted(final, "req", num_req, by)
        origin = (me - by) % num_req
        for_me = jnp.where(source[me] == origin, got, for_me)
        for_mate = jnp.where(source[mate] == origin, got, for_mate)
    crossed = swap_core(for_mate, num_req)
    ckpt = jnp.where(source[me] % 2 == me % 2, for_me, crossed)
    ckpt_states = ckpt.astype(F32).reshape((1, heads, HDIM, STATE))

    extended_x = jnp.concatenate([start_conv[:, :inner], ssm_input], axis=0)
    extended_bc = jnp.concatenate([start_conv[:, inner:], bc_input], axis=0)
    tail = jnp.concatenate(
        [
            lax.dynamic_slice_in_dim(extended_x, my_len, CONV - 1, 0),
            lax.dynamic_slice_in_dim(extended_bc, my_len, CONV - 1, 0),
        ],
        axis=1,
    )
    landed = tail
    for by in range(1, num_req):
        got = shifted(tail, "req", num_req, by)
        landed = jnp.where(source[me] == (me - by) % num_req, got, landed)
    return (mixed, ckpt_states, landed[None, :, :inner], landed[None, :, inner:])


def solution(mesh):
    return jax.shard_map(
        per_device,
        mesh=mesh,
        in_specs=(
            P(("groups", "req"), "tp"),
            P(("groups", "req"), "tp"),
            P(("groups", "req"), None),
            P(("groups", "req"), "tp"),
            P("tp"),
            P("tp"),
            P("tp"),
            P(None, "tp"),
            P(),
            P("tp", None),
            P(("groups", "req"), "tp", None, None),
            P(("groups", "req"), None, "tp"),
            P(("groups", "req"), None, None),
            P("groups"),
            P("groups"),
            P("groups"),
            P("groups"),
        ),
        out_specs=(
            P(("groups", "req"), "tp"),
            P(("groups", "req"), "tp", None, None),
            P(("groups", "req"), None, "tp"),
            P(("groups", "req"), None, None),
        ),
        check_vma=False,
    )
```

```python
import functools

import jax
import jax.numpy as jnp
from jax import lax
from jax.experimental import pallas as pl
from jax.experimental.pallas import tpu as pltpu
from jax.sharding import PartitionSpec as P

HDIM = 64
STATE = 128
GHEADS = 32
CONV = 4
SPAN = 128
SUF = 512
INNER = 8192
BCG = 4
BCW = 1024
NCH = 4
LANES = 128
WIDE = 512
SCAN_WIDE = 1024
PIECES = (2, 2)
VMEM_LIMIT = 56 * 2**20

F32 = jnp.float32
BF16 = jnp.bfloat16
HIGH = lax.Precision.HIGHEST


def wrap(x, n):
    return x & (n - 1) if n & (n - 1) == 0 else x % n


def over(x, n):
    return x >> (n.bit_length() - 1) if n & (n - 1) == 0 else x // n


def silu(x):
    half = 0.5 * x
    return half + half * jnp.tanh(half)


def split_pair(x, heads):
    lane = lax.broadcasted_iota(jnp.int32, x.shape, 1)
    high = x.astype(BF16).astype(F32)
    rest = jnp.where(lane < 2 * heads, x - high, 0.0)
    return jnp.where(lane < heads, high, rest).astype(BF16)


def dot(a, b):
    return jnp.dot(a, b, preferred_element_type=F32)


def dot_t(a, b):
    return lax.dot_general(a, b, (((1,), (1,)), ((), ())), preferred_element_type=F32)


def conv_taps(before, x, weight):
    extended = jnp.concatenate([before, x], axis=0)
    total = extended[8:] * weight[CONV - 1 :]
    for k in range(CONV - 1):
        total += extended[5 + k : 5 + k + SPAN] * weight[k : k + 1]
    return total


def pack_kernel(reqs, meta, px_ref, pb_ref, *conv_refs):
    slots = px_ref.shape[1]
    inner = px_ref.shape[2]
    me = meta[0]
    px = px_ref[...].astype(F32)
    pb = pb_ref[...].astype(F32)
    for by in range(reqs):
        at = jnp.clip(meta[2 + wrap(me + by, reqs)] - slots * me, 0, slots - 1)
        sent_x, sent_b = px[:, 0], pb[:, 0]
        for s in range(1, slots):
            sent_x = jnp.where(at == s, px[:, s], sent_x)
            sent_b = jnp.where(at == s, pb[:, s], sent_b)
        conv_refs[by][:, :inner] = sent_x.astype(BF16)
        conv_refs[by][:, inner:] = sent_b.astype(BF16)


def run_pack(meta, px, pb, reqs):
    taps, _, inner = px.shape
    return pl.pallas_call(
        functools.partial(pack_kernel, reqs),
        grid_spec=pltpu.PrefetchScalarGridSpec(
            num_scalar_prefetch=1,
            grid=(1,),
            in_specs=[
                pl.BlockSpec(px.shape, lambda i, m: (0, 0, 0)),
                pl.BlockSpec(pb.shape, lambda i, m: (0, 0, 0)),
            ],
            out_specs=[pl.BlockSpec((taps, inner + BCW), lambda i, m: (0, 0))] * reqs,
        ),
        out_shape=[jax.ShapeDtypeStruct((taps, inner + BCW), BF16)] * reqs,
        compiler_params=pltpu.CompilerParams(vmem_limit_bytes=VMEM_LIMIT),
        cost_estimate=pl.CostEstimate(flops=10**6, bytes_accessed=2**18, transcendentals=0),
        name="pack",
    )(meta, px, pb)


def choose_kernel(reqs, slots, meta, mine_ref, mate_ref, out_ref, mark_ref):
    slot = meta[2 + wrap(meta[0] + 2 + 2 * pl.program_id(0), reqs)]
    out_ref[...] = jnp.where(over(slot, slots) == meta[0], mine_ref[...], mate_ref[...]).astype(BF16)
    mark_ref[...] = jnp.zeros_like(mark_ref)


def run_choose(meta, mine, mate, reqs):
    slots, inner, _ = mine.shape
    shape = (1, WIDE, STATE)

    def held(meta, by, owner):
        return jnp.clip(meta[2 + wrap(meta[0] + 2 + 2 * by, reqs)] - slots * owner, 0, slots - 1)

    return pl.pallas_call(
        functools.partial(choose_kernel, reqs, slots),
        grid_spec=pltpu.PrefetchScalarGridSpec(
            num_scalar_prefetch=1,
            grid=(reqs // 2 - 1, inner // WIDE),
            in_specs=[
                pl.BlockSpec(shape, lambda i, j, m: (held(m, i, m[0]), j, 0)),
                pl.BlockSpec(shape, lambda i, j, m: (held(m, i, m[0] ^ 1), j, 0)),
            ],
            out_specs=[
                pl.BlockSpec(shape, lambda i, j, m: (i, j, 0)),
                pl.BlockSpec((8, LANES), lambda i, j, m: (0, 0)),
            ],
        ),
        out_shape=[
            jax.ShapeDtypeStruct((reqs // 2 - 1, inner, STATE), BF16),
            jax.ShapeDtypeStruct((8, LANES), F32),
        ],
        compiler_params=pltpu.CompilerParams(vmem_limit_bytes=VMEM_LIMIT),
        cost_estimate=pl.CostEstimate(flops=10**6, bytes_accessed=2 * 2**20, transcendentals=0),
        name="choose",
    )(meta, mine, mate)


def scan_kernel(
    heads,
    slots,
    reqs,
    meta,
    *refs,
):
    scan_body(heads, slots, reqs, meta, refs[:reqs], *refs[reqs + 1 :])


def scan_body(
    heads,
    slots,
    reqs,
    meta,
    conv_refs,
    x_ref,
    b_ref,
    c_ref,
    dt_ref,
    rate_ref,
    skip_ref,
    wx_ref,
    wb_ref,
    wc_ref,
    y_ref,
    final_ref,
    cmap_ref,
    reach_ref,
    total_ref,
    conv_ref,
    pick_ref,
    start,
    state,
    tail_x,
    tail_m,
    left,
    bmap_t,
    factors,
    base,
):
    block = pl.program_id(0)
    c = pl.program_id(1)
    me = meta[0]
    slot = meta[2 + me]
    inner = conv_ref.shape[1] - BCW
    group = over(meta[1] * heads, GHEADS)

    @pl.when((block == 0) & (c == 0))
    def _():
        away = wrap(me - over(slot, slots) + reqs, reqs)
        taken = conv_refs[0][...].astype(F32)
        for by in range(1, reqs):
            taken = jnp.where(away == by, conv_refs[by][...].astype(F32), taken)
        taken = jnp.where(meta[2 + reqs + me] > 0, taken, 0.0)
        start[...] = jnp.concatenate(
            [jnp.zeros((8 - (CONV - 1), inner + BCW), F32), taken], axis=0
        )
        conv_ref[...] = taken.astype(BF16)

    @pl.when(block == 0)
    def _():
        maps = []
        for k, (ref, w) in enumerate(((b_ref, wb_ref), (c_ref, wc_ref))):
            at = pl.multiple_of(inner + (group + k * BCG) * LANES, LANES)
            before = jnp.where(c == 0, start[:, pl.ds(at, LANES)], tail_m[k])
            x = ref[...].astype(F32)
            maps.append(silu(conv_taps(before, x, w[...].astype(F32))).astype(BF16))
            tail_m[k] = x[SPAN - 8 :]
        bmap, cmap = maps
        row = lax.broadcasted_iota(jnp.int32, (SPAN, SPAN), 0)
        col = lax.broadcasted_iota(jnp.int32, (SPAN, SPAN), 1)
        scores = jnp.where(row >= col, dot_t(cmap, bmap), 0.0).astype(BF16)
        left[c, :, :SPAN] = scores
        left[c, :, SPAN:] = cmap
        cmap_ref[...] = cmap
        bmap_t[c] = jnp.transpose(bmap.astype(F32)).astype(BF16)

        @pl.when(c == 0)
        def _():
            base[...] = jnp.zeros_like(base)

        copies = LANES // heads
        logit = jnp.transpose(jnp.concatenate([dt_ref[...]] * copies, axis=0))
        rate = jnp.concatenate([rate_ref[...].reshape(1, heads)] * copies, axis=1)
        skip = jnp.concatenate([skip_ref[...].reshape(1, heads)] * copies, axis=1)
        live = (row + c * SPAN < meta[2 + 3 * reqs + me]).astype(F32)
        step = (jnp.maximum(logit, 0.0) + jnp.log1p(jnp.exp(-jnp.abs(logit)))) * live
        cum = jnp.dot(
            (row >= col).astype(F32),
            -step * rate,
            precision=HIGH,
            preferred_element_type=F32,
        )
        last = cum[SPAN - 1 :]
        mid = 0.5 * last
        factors[c, :SPAN] = split_pair(jnp.exp(cum - mid), heads)
        factors[c, SPAN : 2 * SPAN] = split_pair(jnp.exp(mid - cum) * step, heads)
        before = base[0:1]
        reach_ref[...] = split_pair(jnp.exp(before + cum), heads)
        which = lax.broadcasted_iota(jnp.int32, (16, LANES), 0)
        singles = jnp.where(which == 1, jnp.exp(last - mid), skip)
        factors[c, 2 * SPAN :] = split_pair(jnp.where(which == 0, jnp.exp(mid), singles), heads)
        base[...] = base[...] + last
        total_ref[...] = split_pair(jnp.exp(base[...]), heads)

    @pl.when(c == 0)
    def _():
        state[...] = jnp.zeros_like(state)
        lane = lax.broadcasted_iota(jnp.int32, (LANES, SCAN_WIDE), 0)
        channel = lax.broadcasted_iota(jnp.int32, (LANES, SCAN_WIDE), 1) + block * SCAN_WIDE
        pick_ref[...] = ((wrap(lane, heads) == over(channel, HDIM)) & (lane < 2 * heads)).astype(BF16)
        tail_x[...] = start[:, pl.ds(pl.multiple_of(block * SCAN_WIDE, SCAN_WIDE), SCAN_WIDE)]

    x = x_ref[...].astype(F32)
    conv = conv_taps(tail_x[...], x, wx_ref[...].astype(F32))
    tail_x[...] = x[SPAN - 8 :]
    values = silu(conv).astype(BF16).astype(F32)
    spread = dot(factors[c], pick_ref[...])
    rows = spread[2 * SPAN :]
    scaled = (values * spread[SPAN : 2 * SPAN]).astype(BF16)
    held = state[...] * rows[0:1]
    right = jnp.concatenate([scaled, held.astype(BF16)], axis=0)
    y_ref[...] = dot(left[c], right) * spread[:SPAN] + rows[2:3] * values
    state[...] = (held + dot(bmap_t[c], scaled)) * rows[1:2]

    @pl.when(c == NCH - 1)
    def _():
        final_ref[...] = jnp.transpose(state[...])


def run_scan(meta, conv, mark, x, bc, dt, rate, skip, wx, wbc, heads, slots):
    inner = x.shape[1]
    blocks = inner // SCAN_WIDE
    reqs = len(conv)
    once = lambda b, c: jnp.where(b == 0, c, NCH - 1)
    group = lambda m: over(m[1] * heads, GHEADS)
    in_specs = [pl.BlockSpec((CONV - 1, inner + BCW), lambda b, c, m: (0, 0))] * reqs
    in_specs += [
        pl.BlockSpec((8, LANES), lambda b, c, m: (0, 0)),
        pl.BlockSpec((SPAN, SCAN_WIDE), lambda b, c, m: (c, b)),
        pl.BlockSpec((SPAN, LANES), lambda b, c, m: (once(b, c), group(m))),
        pl.BlockSpec((SPAN, LANES), lambda b, c, m: (once(b, c), group(m) + BCG)),
        pl.BlockSpec((heads, SPAN), lambda b, c, m: (0, once(b, c))),
        pl.BlockSpec((heads,), lambda b, c, m: (0,)),
        pl.BlockSpec((heads,), lambda b, c, m: (0,)),
        pl.BlockSpec((CONV, SCAN_WIDE), lambda b, c, m: (0, b)),
        pl.BlockSpec((CONV, LANES), lambda b, c, m: (0, group(m))),
        pl.BlockSpec((CONV, LANES), lambda b, c, m: (0, group(m) + BCG)),
    ]
    out_specs = [
        pl.BlockSpec((SPAN, SCAN_WIDE), lambda b, c, m: (c, b)),
        pl.BlockSpec((SCAN_WIDE, STATE), lambda b, c, m: (b, 0)),
        pl.BlockSpec((SPAN, LANES), lambda b, c, m: (once(b, c), 0)),
        pl.BlockSpec((SPAN, LANES), lambda b, c, m: (once(b, c), 0)),
        pl.BlockSpec((16, LANES), lambda b, c, m: (0, 0)),
        pl.BlockSpec((CONV - 1, inner + BCW), lambda b, c, m: (0, 0)),
        pl.BlockSpec((LANES, SCAN_WIDE), lambda b, c, m: (0, b)),
    ]
    return pl.pallas_call(
        functools.partial(scan_kernel, heads, slots, reqs),
        grid_spec=pltpu.PrefetchScalarGridSpec(
            num_scalar_prefetch=1,
            grid=(blocks, NCH),
            in_specs=in_specs,
            out_specs=out_specs,
            scratch_shapes=[
                pltpu.VMEM((8, inner + BCW), F32),
                pltpu.VMEM((STATE, SCAN_WIDE), F32),
                pltpu.VMEM((8, SCAN_WIDE), F32),
                pltpu.VMEM((2, 8, LANES), F32),
                pltpu.VMEM((NCH, SPAN, 2 * SPAN), BF16),
                pltpu.VMEM((NCH, STATE, SPAN), BF16),
                pltpu.VMEM((NCH, 2 * SPAN + 16, LANES), BF16),
                pltpu.VMEM((16, LANES), F32),
            ],
        ),
        out_shape=[
            jax.ShapeDtypeStruct((SUF, inner), F32),
            jax.ShapeDtypeStruct((inner, STATE), F32),
            jax.ShapeDtypeStruct((SUF, LANES), BF16),
            jax.ShapeDtypeStruct((SUF, LANES), BF16),
            jax.ShapeDtypeStruct((16, LANES), BF16),
            jax.ShapeDtypeStruct((CONV - 1, inner + BCW), BF16),
            jax.ShapeDtypeStruct((LANES, inner), BF16),
        ],
        compiler_params=pltpu.CompilerParams(
            dimension_semantics=("arbitrary", "arbitrary"), vmem_limit_bytes=VMEM_LIMIT
        ),
        cost_estimate=pl.CostEstimate(
            flops=8 * 10**9, bytes_accessed=12 * 2**20, transcendentals=SUF * inner
        ),
        name="local_scan",
    )(meta, *conv, mark, x, bc, bc, dt, rate, skip, wx, wbc, wbc)


def project_kernel(chunks, shares, picks, meta, *refs):
    if picks:
        reqs, slots = picks
        others = reqs // 2 - 1
        mine_ref, mate_ref = refs[:2]
        got_refs = refs[2 : 2 + others]
        refs = refs[2 + others :]
    else:
        start_ref, refs = refs[0], refs[1:]
    y_ref, gate_ref, cmap_ref, reach_ref, gain_ref, pick_ref, w_ref = refs[:7]
    out_refs = refs[7 : 7 + shares]
    sq_ref = refs[7 + shares]
    if picks:
        start_ref = refs[8 + shares]
    held, w_held, arrived = refs[-3:]
    step = pl.program_id(0)
    inner = y_ref.shape[1]
    share = out_refs[0].shape[1]

    def fetch(q):
        column = pl.multiple_of(wrap(q + meta[1], shares) * share, share)
        return pltpu.make_async_copy(
            w_ref.at[:, pl.ds(column, share)], w_held.at[q], arrived.at[q]
        )

    @pl.when(step == 0)
    def _():
        for q in range(shares):
            fetch(q).start()

    if picks:

        @pl.when(step == 0)
        def _():
            me = meta[0]
            owner = over(meta[2 + me], slots)
            away = wrap(over(me, 2) - over(owner, 2) + reqs // 2, reqs // 2)
            taken = jnp.where(owner == me, mine_ref[0], mate_ref[0])
            for k in range(others):
                taken = jnp.where(away == k + 1, got_refs[k][0].astype(F32), taken)
            start_ref[...] = jnp.where(meta[2 + reqs + me] > 0, taken, 0.0).astype(BF16)

    @pl.when(step < chunks)
    def _():
        squares = jnp.zeros((SPAN, LANES), F32)
        rows = pl.ds(pl.multiple_of(step * SPAN, SPAN), SPAN)
        for i in range(inner // WIDE):
            at = pl.ds(i * WIDE, WIDE)
            carried = dot_t(cmap_ref[...], start_ref[at, :])
            y = y_ref[:, at] + dot(reach_ref[...], pick_ref[:, at]) * carried
            gated = y * silu(gate_ref[:, at].astype(F32))
            held[rows, at] = (gated * gain_ref[:, at]).astype(BF16)
            gated = gated * gated
            for j in range(WIDE // LANES):
                squares += gated[:, j * LANES : (j + 1) * LANES]
        sq_ref[...] = lax.dot_general(
            jnp.ones((8, LANES), F32),
            squares,
            (((1,), (1,)), ((), ())),
            precision=HIGH,
            preferred_element_type=F32,
        )

    for q in range(shares):

        @pl.when(step == chunks + q)
        def _(q=q):
            fetch(q).wait()
            out_refs[q][...] = dot(held[...], w_held[q]).astype(BF16)


def run_project(first, chunks, meta, states, y, gate, cmap, reach, gain, pick, weight, shares, reqs):
    inner, width = weight.shape
    share = width // shares
    count = chunks * SPAN
    rows = lambda n, m: (first + jnp.minimum(n, chunks - 1), 0)
    whole = lambda n, m: (0, 0)
    state = (1, inner, STATE)
    choose = len(states) > 1
    slots = states[0].shape[0]

    def held(owner, m):
        return jnp.clip(m[2 + m[0]] - slots * owner, 0, slots - 1)

    if choose:
        state_specs = [
            pl.BlockSpec(state, lambda n, m: (held(m[0], m), 0, 0)),
            pl.BlockSpec(state, lambda n, m: (held(m[0] ^ 1, m), 0, 0)),
        ] + [pl.BlockSpec(state, lambda n, m: (0, 0, 0))] * (len(states) - 2)
    else:
        state_specs = [pl.BlockSpec((inner, STATE), whole)]
    out_specs = [
        pl.BlockSpec((count, share), whole)
        for q in range(shares)
    ] + [pl.BlockSpec((8, LANES), lambda n, m: (0, jnp.minimum(n, chunks - 1)))]
    out_shape = [jax.ShapeDtypeStruct((count, share), BF16)] * shares + [
        jax.ShapeDtypeStruct((8, count), F32)
    ]
    if choose:
        out_specs.append(pl.BlockSpec((inner, STATE), whole))
        out_shape.append(jax.ShapeDtypeStruct((inner, STATE), BF16))
    return pl.pallas_call(
        functools.partial(project_kernel, chunks, shares, (reqs, slots) if choose else None),
        grid_spec=pltpu.PrefetchScalarGridSpec(
            num_scalar_prefetch=1,
            grid=(chunks + shares,),
            in_specs=state_specs
            + [
                pl.BlockSpec((SPAN, inner), rows),
                pl.BlockSpec((SPAN, inner), rows),
                pl.BlockSpec((SPAN, LANES), rows),
                pl.BlockSpec((SPAN, LANES), rows),
                pl.BlockSpec((1, inner), whole),
                pl.BlockSpec((LANES, inner), whole),
                pl.BlockSpec(memory_space=pl.ANY),
            ],
            out_specs=out_specs,
            scratch_shapes=[
                pltpu.VMEM((count, inner), BF16),
                pltpu.VMEM((shares, inner, share), BF16),
                pltpu.SemaphoreType.DMA((shares,)),
            ],
        ),
        out_shape=out_shape,
        compiler_params=pltpu.CompilerParams(
            dimension_semantics=("arbitrary",), vmem_limit_bytes=VMEM_LIMIT
        ),
        cost_estimate=pl.CostEstimate(
            flops=2 * count * inner * width,
            bytes_accessed=2 * inner * width + 10 * 2**20,
            transcendentals=count * inner,
        ),
        name="project",
    )(meta, *states, y, gate, cmap, reach, gain, pick, weight)


def line_sums(parts, size):
    to_right = [(i, i + 1) for i in range(size - 1)]
    to_left = [(i + 1, i) for i in range(size - 1)]
    add = lambda a, b: (a.astype(F32) + b.astype(F32)).astype(BF16)
    right = [None] * len(parts)
    left = [None] * len(parts)
    for s in range(size - 1):
        for p, part in enumerate(parts):
            go_right, go_left = part[size - 1 - s], part[s + 1]
            if s:
                if p + 1 < len(parts) and s == 1:
                    right[p], left[p], _ = lax.optimization_barrier(
                        (right[p], left[p], parts[p + 1][0])
                    )
                go_right, go_left = add(go_right, right[p]), add(go_left, left[p])
            right[p] = lax.ppermute(go_right, "tp", to_right[: s + 1])
            left[p] = lax.ppermute(go_left, "tp", to_left[size - 2 - s :])
    return [
        part[0].astype(F32) + r.astype(F32) + l.astype(F32)
        for part, r, l in zip(parts, right, left)
    ]


def source_of(meta, device, reqs):
    found = jnp.int32(0)
    for r in range(reqs):
        found += jnp.where(meta[2 + 2 * reqs + r] == device, r, 0)
    return found


def ending_kernel(reqs, meta, mark_ref, local_ref, start_ref, total_ref, pick_ref, conv_ref, x_ref, bc_ref, out_ref):
    inner = local_ref.shape[0]
    length = meta[2 + 3 * reqs + meta[0]]
    for i in range(inner // WIDE):
        at = pl.ds(i * WIDE, WIDE)
        decay = dot(total_ref[...], pick_ref[:, at])[0:1]
        decay = jnp.transpose(jnp.broadcast_to(decay, (STATE, WIDE)))
        out_ref[at, :] = (local_ref[at, :] + decay * start_ref[at, :].astype(F32)).astype(BF16)
    row = lax.broadcasted_iota(jnp.int32, (16, SUF), 0) + length - (CONV - 1)
    found = (row == lax.broadcasted_iota(jnp.int32, (16, SUF), 1)).astype(BF16)
    conv = conv_ref[...].astype(F32)
    row = lax.broadcasted_iota(jnp.int32, (16, WIDE), 0) + length
    for i in range((inner + BCW) // WIDE):
        at = i * WIDE
        source = x_ref[:, at : at + WIDE] if at < inner else bc_ref[:, at - inner : at - inner + WIDE]
        tail = dot(found, source)
        for k in range(CONV - 1):
            tail += jnp.where(row == k, conv[k : k + 1, at : at + WIDE], 0.0)
        tail = tail.astype(BF16)
        for j in range(WIDE // LANES):
            to = inner + (at // LANES + j) * 16
            out_ref[to : to + 16, :] = tail[:, j * LANES : (j + 1) * LANES]


def run_ending(meta, mark, local, start, total, pick, conv, x, bc, reqs):
    inner = local.shape[0]
    rows = inner + (inner + BCW) // LANES * 16
    operands = (mark, local, start, total, pick, conv, x, bc)
    return pl.pallas_call(
        functools.partial(ending_kernel, reqs),
        grid_spec=pltpu.PrefetchScalarGridSpec(
            num_scalar_prefetch=1,
            grid=(1,),
            in_specs=[pl.BlockSpec(a.shape, lambda i, m: (0, 0)) for a in operands],
            out_specs=pl.BlockSpec((rows, LANES), lambda i, m: (0, 0)),
        ),
        out_shape=jax.ShapeDtypeStruct((rows, LANES), BF16),
        compiler_params=pltpu.CompilerParams(vmem_limit_bytes=VMEM_LIMIT),
        cost_estimate=pl.CostEstimate(flops=10**8, bytes_accessed=6 * 2**20, transcendentals=0),
        name="ending",
    )(meta, *operands)


def route_kernel(reqs, meta, *refs):
    origin = over(source_of(meta, meta[0] ^ 1, reqs), 2)
    away = wrap(over(meta[0], 2) - origin + reqs // 2, reqs // 2)
    taken = refs[0][...]
    for k in range(1, reqs // 2):
        taken = jnp.where(away == k, refs[k][...], taken)
    refs[-1][...] = taken


def run_route(meta, ends, reqs):
    shape = ends[0].shape
    return pl.pallas_call(
        functools.partial(route_kernel, reqs),
        grid_spec=pltpu.PrefetchScalarGridSpec(
            num_scalar_prefetch=1,
            grid=(1,),
            in_specs=[pl.BlockSpec(shape, lambda i, m: (0, 0))] * len(ends),
            out_specs=pl.BlockSpec(shape, lambda i, m: (0, 0)),
        ),
        out_shape=jax.ShapeDtypeStruct(shape, BF16),
        compiler_params=pltpu.CompilerParams(vmem_limit_bytes=VMEM_LIMIT),
        cost_estimate=pl.CostEstimate(flops=10**6, bytes_accessed=2 * 2**20, transcendentals=0),
        name="route",
    )(meta, *ends)


def land_kernel(reqs, meta, *refs):
    state_ref, x_ref, bc_ref = refs[-3:]
    crossed_ref = refs[-4]
    source = source_of(meta, meta[0], reqs)
    away = wrap(over(meta[0], 2) - over(source, 2) + reqs // 2, reqs // 2)
    inner = state_ref.shape[0]

    def taken(at):
        value = refs[0][at, :]
        for k in range(1, reqs // 2):
            value = jnp.where(away == k, refs[k][at, :], value)
        return jnp.where((source & 1) == (meta[0] & 1), value, crossed_ref[at, :])

    for i in range(inner // WIDE):
        at = pl.ds(i * WIDE, WIDE)
        state_ref[at, :] = taken(at).astype(F32)
    tiles = (inner + BCW) // LANES
    tails = [taken(pl.ds(inner + j * 16, 16))[: CONV - 1] for j in range(tiles)]
    x_ref[...] = jnp.concatenate(tails[: inner // LANES], axis=1)
    bc_ref[...] = jnp.concatenate(tails[inner // LANES :], axis=1)


def run_land(meta, ends, crossed, inner, reqs):
    shape = crossed.shape
    outs = [(inner, STATE), (CONV - 1, inner), (CONV - 1, BCW)]
    return pl.pallas_call(
        functools.partial(land_kernel, reqs),
        grid_spec=pltpu.PrefetchScalarGridSpec(
            num_scalar_prefetch=1,
            grid=(1,),
            in_specs=[pl.BlockSpec(shape, lambda i, m: (0, 0))] * (len(ends) + 1),
            out_specs=[pl.BlockSpec(o, lambda i, m: (0, 0)) for o in outs],
        ),
        out_shape=[jax.ShapeDtypeStruct(o, t) for o, t in zip(outs, (F32, BF16, BF16))],
        compiler_params=pltpu.CompilerParams(vmem_limit_bytes=VMEM_LIMIT),
        cost_estimate=pl.CostEstimate(flops=10**6, bytes_accessed=3 * 2**20, transcendentals=0),
        name="land",
    )(meta, *ends, crossed)


def shifted(x, axis, size, by):
    return lax.ppermute(x, axis, [(i, (i + by) % size) for i in range(size)])


def swap_core(x, size):
    return lax.ppermute(x, "req", [(i, i ^ 1) for i in range(size)])


def per_device(
    ssm_input,
    gate_input,
    bc_input,
    dt_input,
    decay_rate,
    skip_gain,
    norm_gain,
    conv_x_weight,
    conv_bc_weight,
    out_weight,
    pool_states,
    pool_conv_x,
    pool_conv_bc,
    prefix_slot,
    prefix_spans,
    dest_slot,
    suffix_len,
):
    num_req = lax.axis_size("req")
    num_tp = lax.axis_size("tp")
    me = lax.axis_index("req")
    z = lax.axis_index("tp")
    heads = dt_input.shape[1]
    inner = ssm_input.shape[1]
    slots = pool_states.shape[0]
    meta = jnp.concatenate(
        [jnp.stack([me, z]), prefix_slot, prefix_spans, dest_slot, suffix_len]
    ).astype(jnp.int32)

    mine = pool_states.reshape(slots, inner, STATE)
    other = swap_core(mine, num_req)
    conv = run_pack(
        meta,
        jnp.transpose(pool_conv_x, (1, 0, 2)),
        jnp.transpose(pool_conv_bc, (1, 0, 2)),
        num_req,
    )
    convs = [conv[0]] + [shifted(conv[by], "req", num_req, by) for by in range(1, num_req)]
    chosen, mark = run_choose(meta, mine, other, num_req)
    got = [
        shifted(chosen[k : k + 1], "req", num_req, 2 * k + 2) for k in range(num_req // 2 - 1)
    ]

    y_local, local_final, cmap, reach, total, start_conv, pick = run_scan(
        meta,
        convs,
        mark,
        ssm_input,
        bc_input,
        dt_input.T,
        decay_rate,
        skip_gain,
        conv_x_weight,
        conv_bc_weight,
        heads,
        slots,
    )
    states = [mine, other] + got
    parts, squares = [], []
    first = 0
    for chunks in PIECES:
        result = run_project(
            first,
            chunks,
            meta,
            states,
            y_local,
            gate_input,
            cmap,
            reach,
            norm_gain[None, :],
            pick,
            out_weight,
            num_tp,
            num_req,
        )
        first += chunks
        parts.append(result[:num_tp])
        squares.append(result[num_tp][0])
        if len(states) > 1:
            start = result[num_tp + 1]
            states = [start]
    summed = jnp.concatenate(line_sums(parts, num_tp), axis=0)

    my_len = suffix_len[me]
    square = jnp.concatenate(squares)
    square_total = square
    for by in range(1, num_tp):
        square_total = square_total + shifted(square, "tp", num_tp, by)
    scale = lax.rsqrt(square_total / INNER + 1e-05)
    scale = jnp.where(jnp.arange(SUF) < my_len, scale, 0.0)
    mixed = (summed * scale[:, None]).astype(BF16)

    end = run_ending(
        meta, result[num_tp], local_final, start, total, pick, start_conv, ssm_input, bc_input, num_req
    )
    ends = [end] + [shifted(end, "req", num_req, by) for by in range(2, num_req, 2)]
    crossed = swap_core(run_route(meta, ends, num_req), num_req)
    ckpt_states, ckpt_x, ckpt_bc = run_land(meta, ends, crossed, inner, num_req)
    return (
        mixed,
        ckpt_states.reshape((1, heads, HDIM, STATE)),
        ckpt_x[None],
        ckpt_bc[None],
    )


def solution(mesh):
    return jax.shard_map(
        per_device,
        mesh=mesh,
        in_specs=(
            P(("groups", "req"), "tp"),
            P(("groups", "req"), "tp"),
            P(("groups", "req"), None),
            P(("groups", "req"), "tp"),
            P("tp"),
            P("tp"),
            P("tp"),
            P(None, "tp"),
            P(),
            P("tp", None),
            P(("groups", "req"), "tp", None, None),
            P(("groups", "req"), None, "tp"),
            P(("groups", "req"), None, None),
            P("groups"),
            P("groups"),
            P("groups"),
            P("groups"),
        ),
        out_specs=(
            P(("groups", "req"), "tp"),
            P(("groups", "req"), "tp", None, None),
            P(("groups", "req"), None, "tp"),
            P(("groups", "req"), None, None),
        ),
        check_vma=False,
    )
```

```python
import functools

import jax
import jax.numpy as jnp
from jax import lax
from jax.experimental import pallas as pl
from jax.experimental.pallas import tpu as pltpu
from jax.sharding import PartitionSpec as P

HDIM = 64
STATE = 128
GHEADS = 32
CONV = 4
SPAN = 128
SUF = 512
INNER = 8192
BCG = 4
BCW = 1024
NCH = 4
LANES = 128
WIDE = 512
SCAN_WIDE = 1024
PIECES = (2, 2)

F32 = jnp.float32
BF16 = jnp.bfloat16
HIGH = lax.Precision.HIGHEST


def wrap(x, n):
    return x & (n - 1) if n & (n - 1) == 0 else x % n


def over(x, n):
    return x >> (n.bit_length() - 1) if n & (n - 1) == 0 else x // n


def silu(x):
    half = 0.5 * x
    return half + half * jnp.tanh(half)


def split_pair(x, heads):
    lane = lax.broadcasted_iota(jnp.int32, x.shape, 1)
    high = x.astype(BF16).astype(F32)
    rest = jnp.where(lane < 2 * heads, x - high, 0.0)
    return jnp.where(lane < heads, high, rest).astype(BF16)


def dot(a, b):
    return jnp.dot(a, b, preferred_element_type=F32)


def dot_t(a, b):
    return lax.dot_general(a, b, (((1,), (1,)), ((), ())), preferred_element_type=F32)


def conv_taps(before, x, weight):
    extended = jnp.concatenate([before, x], axis=0)
    total = extended[8:] * weight[CONV - 1 :]
    for k in range(CONV - 1):
        total += extended[5 + k : 5 + k + SPAN] * weight[k : k + 1]
    return total


def pack_kernel(reqs, meta, px_ref, pb_ref, *conv_refs):
    slots = px_ref.shape[1]
    inner = px_ref.shape[2]
    me = meta[0]
    px = px_ref[...].astype(F32)
    pb = pb_ref[...].astype(F32)
    for by in range(reqs):
        at = jnp.clip(meta[2 + wrap(me + by, reqs)] - slots * me, 0, slots - 1)
        sent_x, sent_b = px[:, 0], pb[:, 0]
        for s in range(1, slots):
            sent_x = jnp.where(at == s, px[:, s], sent_x)
            sent_b = jnp.where(at == s, pb[:, s], sent_b)
        conv_refs[by][:, :inner] = sent_x.astype(BF16)
        conv_refs[by][:, inner:] = sent_b.astype(BF16)


def run_pack(meta, px, pb, reqs):
    taps, _, inner = px.shape
    return pl.pallas_call(
        functools.partial(pack_kernel, reqs),
        grid_spec=pltpu.PrefetchScalarGridSpec(
            num_scalar_prefetch=1,
            grid=(1,),
            in_specs=[
                pl.BlockSpec(px.shape, lambda i, m: (0, 0, 0)),
                pl.BlockSpec(pb.shape, lambda i, m: (0, 0, 0)),
            ],
            out_specs=[pl.BlockSpec((taps, inner + BCW), lambda i, m: (0, 0))] * reqs,
        ),
        out_shape=[jax.ShapeDtypeStruct((taps, inner + BCW), BF16)] * reqs,
        compiler_params=pltpu.CompilerParams(vmem_limit_bytes=8 * 2**20),
        cost_estimate=pl.CostEstimate(flops=10**6, bytes_accessed=2**18, transcendentals=0),
        name="pack",
    )(meta, px, pb)


def choose_kernel(reqs, slots, meta, mine_ref, mate_ref, out_ref, mark_ref):
    slot = meta[2 + wrap(meta[0] + 2 + 2 * pl.program_id(0), reqs)]
    out_ref[...] = jnp.where(over(slot, slots) == meta[0], mine_ref[...], mate_ref[...]).astype(BF16)
    mark_ref[...] = jnp.zeros_like(mark_ref)


def run_choose(meta, mine, mate, reqs):
    slots, inner, _ = mine.shape
    shape = (1, WIDE, STATE)

    def held(meta, by, owner):
        return jnp.clip(meta[2 + wrap(meta[0] + 2 + 2 * by, reqs)] - slots * owner, 0, slots - 1)

    return pl.pallas_call(
        functools.partial(choose_kernel, reqs, slots),
        grid_spec=pltpu.PrefetchScalarGridSpec(
            num_scalar_prefetch=1,
            grid=(reqs // 2 - 1, inner // WIDE),
            in_specs=[
                pl.BlockSpec(shape, lambda i, j, m: (held(m, i, m[0]), j, 0)),
                pl.BlockSpec(shape, lambda i, j, m: (held(m, i, m[0] ^ 1), j, 0)),
            ],
            out_specs=[
                pl.BlockSpec(shape, lambda i, j, m: (i, j, 0)),
                pl.BlockSpec((8, LANES), lambda i, j, m: (0, 0)),
            ],
        ),
        out_shape=[
            jax.ShapeDtypeStruct((reqs // 2 - 1, inner, STATE), BF16),
            jax.ShapeDtypeStruct((8, LANES), F32),
        ],
        compiler_params=pltpu.CompilerParams(vmem_limit_bytes=8 * 2**20),
        cost_estimate=pl.CostEstimate(flops=10**6, bytes_accessed=2 * 2**20, transcendentals=0),
        name="choose",
    )(meta, mine, mate)


def scan_kernel(
    heads,
    slots,
    reqs,
    meta,
    *refs,
):
    scan_body(heads, slots, reqs, meta, refs[:reqs], *refs[reqs + 1 :])


def scan_body(
    heads,
    slots,
    reqs,
    meta,
    conv_refs,
    x_ref,
    b_ref,
    c_ref,
    dt_ref,
    rate_ref,
    skip_ref,
    wx_ref,
    wb_ref,
    wc_ref,
    y_ref,
    final_ref,
    cmap_ref,
    reach_ref,
    total_ref,
    conv_ref,
    pick_ref,
    start,
    state,
    tail_x,
    tail_m,
    left,
    bmap_t,
    factors,
    base,
):
    block = pl.program_id(0)
    c = pl.program_id(1)
    me = meta[0]
    slot = meta[2 + me]
    inner = conv_ref.shape[1] - BCW
    group = over(meta[1] * heads, GHEADS)

    @pl.when((block == 0) & (c == 0))
    def _():
        away = wrap(me - over(slot, slots) + reqs, reqs)
        taken = conv_refs[0][...].astype(F32)
        for by in range(1, reqs):
            taken = jnp.where(away == by, conv_refs[by][...].astype(F32), taken)
        taken = jnp.where(meta[2 + reqs + me] > 0, taken, 0.0)
        start[...] = jnp.concatenate(
            [jnp.zeros((8 - (CONV - 1), inner + BCW), F32), taken], axis=0
        )
        conv_ref[...] = taken.astype(BF16)

    @pl.when(block == 0)
    def _():
        maps = []
        for k, (ref, w) in enumerate(((b_ref, wb_ref), (c_ref, wc_ref))):
            at = pl.multiple_of(inner + (group + k * BCG) * LANES, LANES)
            before = jnp.where(c == 0, start[:, pl.ds(at, LANES)], tail_m[k])
            x = ref[...].astype(F32)
            maps.append(silu(conv_taps(before, x, w[...].astype(F32))).astype(BF16))
            tail_m[k] = x[SPAN - 8 :]
        bmap, cmap = maps
        row = lax.broadcasted_iota(jnp.int32, (SPAN, SPAN), 0)
        col = lax.broadcasted_iota(jnp.int32, (SPAN, SPAN), 1)
        scores = jnp.where(row >= col, dot_t(cmap, bmap), 0.0).astype(BF16)
        left[c, :, :SPAN] = scores
        left[c, :, SPAN:] = cmap
        cmap_ref[...] = cmap
        bmap_t[c] = jnp.transpose(bmap.astype(F32)).astype(BF16)

        @pl.when(c == 0)
        def _():
            base[...] = jnp.zeros_like(base)

        copies = LANES // heads
        logit = jnp.transpose(jnp.concatenate([dt_ref[...]] * copies, axis=0))
        rate = jnp.concatenate([rate_ref[...].reshape(1, heads)] * copies, axis=1)
        skip = jnp.concatenate([skip_ref[...].reshape(1, heads)] * copies, axis=1)
        live = (row + c * SPAN < meta[2 + 3 * reqs + me]).astype(F32)
        step = (jnp.maximum(logit, 0.0) + jnp.log1p(jnp.exp(-jnp.abs(logit)))) * live
        cum = jnp.dot(
            (row >= col).astype(F32),
            -step * rate,
            precision=HIGH,
            preferred_element_type=F32,
        )
        last = cum[SPAN - 1 :]
        mid = 0.5 * last
        factors[c, :SPAN] = split_pair(jnp.exp(cum - mid), heads)
        factors[c, SPAN : 2 * SPAN] = split_pair(jnp.exp(mid - cum) * step, heads)
        before = base[0:1]
        reach_ref[...] = split_pair(jnp.exp(before + cum), heads)
        which = lax.broadcasted_iota(jnp.int32, (16, LANES), 0)
        singles = jnp.where(which == 1, jnp.exp(last - mid), skip)
        factors[c, 2 * SPAN :] = split_pair(jnp.where(which == 0, jnp.exp(mid), singles), heads)
        base[...] = base[...] + last
        total_ref[...] = split_pair(jnp.exp(base[...]), heads)

    @pl.when(c == 0)
    def _():
        state[...] = jnp.zeros_like(state)
        lane = lax.broadcasted_iota(jnp.int32, (LANES, SCAN_WIDE), 0)
        channel = lax.broadcasted_iota(jnp.int32, (LANES, SCAN_WIDE), 1) + block * SCAN_WIDE
        pick_ref[...] = ((wrap(lane, heads) == over(channel, HDIM)) & (lane < 2 * heads)).astype(BF16)
        tail_x[...] = start[:, pl.ds(pl.multiple_of(block * SCAN_WIDE, SCAN_WIDE), SCAN_WIDE)]

    x = x_ref[...].astype(F32)
    conv = conv_taps(tail_x[...], x, wx_ref[...].astype(F32))
    tail_x[...] = x[SPAN - 8 :]
    values = silu(conv).astype(BF16).astype(F32)
    spread = dot(factors[c], pick_ref[...])
    rows = spread[2 * SPAN :]
    scaled = (values * spread[SPAN : 2 * SPAN]).astype(BF16)
    held = state[...] * rows[0:1]
    right = jnp.concatenate([scaled, held.astype(BF16)], axis=0)
    y_ref[...] = dot(left[c], right) * spread[:SPAN] + rows[2:3] * values
    state[...] = (held + dot(bmap_t[c], scaled)) * rows[1:2]

    @pl.when(c == NCH - 1)
    def _():
        final_ref[...] = jnp.transpose(state[...])


def run_scan(meta, conv, mark, x, bc, dt, rate, skip, wx, wbc, heads, slots):
    inner = x.shape[1]
    blocks = inner // SCAN_WIDE
    reqs = len(conv)
    once = lambda b, c: jnp.where(b == 0, c, NCH - 1)
    group = lambda m: over(m[1] * heads, GHEADS)
    in_specs = [pl.BlockSpec((CONV - 1, inner + BCW), lambda b, c, m: (0, 0))] * reqs
    in_specs += [
        pl.BlockSpec((8, LANES), lambda b, c, m: (0, 0)),
        pl.BlockSpec((SPAN, SCAN_WIDE), lambda b, c, m: (c, b)),
        pl.BlockSpec((SPAN, LANES), lambda b, c, m: (once(b, c), group(m))),
        pl.BlockSpec((SPAN, LANES), lambda b, c, m: (once(b, c), group(m) + BCG)),
        pl.BlockSpec((heads, SPAN), lambda b, c, m: (0, once(b, c))),
        pl.BlockSpec((heads,), lambda b, c, m: (0,)),
        pl.BlockSpec((heads,), lambda b, c, m: (0,)),
        pl.BlockSpec((CONV, SCAN_WIDE), lambda b, c, m: (0, b)),
        pl.BlockSpec((CONV, LANES), lambda b, c, m: (0, group(m))),
        pl.BlockSpec((CONV, LANES), lambda b, c, m: (0, group(m) + BCG)),
    ]
    out_specs = [
        pl.BlockSpec((SPAN, SCAN_WIDE), lambda b, c, m: (c, b)),
        pl.BlockSpec((SCAN_WIDE, STATE), lambda b, c, m: (b, 0)),
        pl.BlockSpec((SPAN, LANES), lambda b, c, m: (once(b, c), 0)),
        pl.BlockSpec((SPAN, LANES), lambda b, c, m: (once(b, c), 0)),
        pl.BlockSpec((16, LANES), lambda b, c, m: (0, 0)),
        pl.BlockSpec((CONV - 1, inner + BCW), lambda b, c, m: (0, 0)),
        pl.BlockSpec((LANES, SCAN_WIDE), lambda b, c, m: (0, b)),
    ]
    return pl.pallas_call(
        functools.partial(scan_kernel, heads, slots, reqs),
        grid_spec=pltpu.PrefetchScalarGridSpec(
            num_scalar_prefetch=1,
            grid=(blocks, NCH),
            in_specs=in_specs,
            out_specs=out_specs,
            scratch_shapes=[
                pltpu.VMEM((8, inner + BCW), F32),
                pltpu.VMEM((STATE, SCAN_WIDE), F32),
                pltpu.VMEM((8, SCAN_WIDE), F32),
                pltpu.VMEM((2, 8, LANES), F32),
                pltpu.VMEM((NCH, SPAN, 2 * SPAN), BF16),
                pltpu.VMEM((NCH, STATE, SPAN), BF16),
                pltpu.VMEM((NCH, 2 * SPAN + 16, LANES), BF16),
                pltpu.VMEM((16, LANES), F32),
            ],
        ),
        out_shape=[
            jax.ShapeDtypeStruct((SUF, inner), F32),
            jax.ShapeDtypeStruct((inner, STATE), F32),
            jax.ShapeDtypeStruct((SUF, LANES), BF16),
            jax.ShapeDtypeStruct((SUF, LANES), BF16),
            jax.ShapeDtypeStruct((16, LANES), BF16),
            jax.ShapeDtypeStruct((CONV - 1, inner + BCW), BF16),
            jax.ShapeDtypeStruct((LANES, inner), BF16),
        ],
        compiler_params=pltpu.CompilerParams(
            dimension_semantics=("arbitrary", "arbitrary"), vmem_limit_bytes=24 * 2**20
        ),
        cost_estimate=pl.CostEstimate(
            flops=8 * 10**9, bytes_accessed=12 * 2**20, transcendentals=SUF * inner
        ),
        name="local_scan",
    )(meta, *conv, mark, x, bc, bc, dt, rate, skip, wx, wbc, wbc)


def project_kernel(chunks, shares, picks, meta, *refs):
    if picks:
        reqs, slots = picks
        others = reqs // 2 - 1
        mine_ref, mate_ref = refs[:2]
        got_refs = refs[2 : 2 + others]
        refs = refs[2 + others :]
    else:
        start_ref, refs = refs[0], refs[1:]
    y_ref, gate_ref, cmap_ref, reach_ref, gain_ref, pick_ref, w_ref = refs[:7]
    out_refs = refs[7 : 7 + shares]
    sq_ref = refs[7 + shares]
    if picks:
        start_ref = refs[8 + shares]
    held, w_held, arrived = refs[-3:]
    step = pl.program_id(0)
    inner = y_ref.shape[1]
    share = out_refs[0].shape[1]

    def fetch(q):
        column = pl.multiple_of(wrap(q + meta[1], shares) * share, share)
        return pltpu.make_async_copy(
            w_ref.at[:, pl.ds(column, share)], w_held.at[q], arrived.at[q]
        )

    @pl.when(step == 0)
    def _():
        for q in range(shares):
            fetch(q).start()

    if picks:

        @pl.when(step == 0)
        def _():
            me = meta[0]
            owner = over(meta[2 + me], slots)
            away = wrap(over(me, 2) - over(owner, 2) + reqs // 2, reqs // 2)
            taken = jnp.where(owner == me, mine_ref[0], mate_ref[0])
            for k in range(others):
                taken = jnp.where(away == k + 1, got_refs[k][0].astype(F32), taken)
            start_ref[...] = jnp.where(meta[2 + reqs + me] > 0, taken, 0.0).astype(BF16)

    @pl.when(step < chunks)
    def _():
        squares = jnp.zeros((SPAN, LANES), F32)
        rows = pl.ds(pl.multiple_of(step * SPAN, SPAN), SPAN)
        for i in range(inner // WIDE):
            at = pl.ds(i * WIDE, WIDE)
            carried = dot_t(cmap_ref[...], start_ref[at, :])
            y = y_ref[:, at] + dot(reach_ref[...], pick_ref[:, at]) * carried
            gated = y * silu(gate_ref[:, at].astype(F32))
            held[rows, at] = (gated * gain_ref[:, at]).astype(BF16)
            gated = gated * gated
            for j in range(WIDE // LANES):
                squares += gated[:, j * LANES : (j + 1) * LANES]
        sq_ref[...] = lax.dot_general(
            jnp.ones((8, LANES), F32),
            squares,
            (((1,), (1,)), ((), ())),
            precision=HIGH,
            preferred_element_type=F32,
        )

    for q in range(shares):

        @pl.when(step == chunks + q)
        def _(q=q):
            fetch(q).wait()
            out_refs[q][...] = dot(held[...], w_held[q]).astype(BF16)


def run_project(first, chunks, meta, states, y, gate, cmap, reach, gain, pick, weight, shares, reqs):
    inner, width = weight.shape
    share = width // shares
    count = chunks * SPAN
    rows = lambda n, m: (first + jnp.minimum(n, chunks - 1), 0)
    whole = lambda n, m: (0, 0)
    state = (1, inner, STATE)
    choose = len(states) > 1
    slots = states[0].shape[0]

    def held(owner, m):
        return jnp.clip(m[2 + m[0]] - slots * owner, 0, slots - 1)

    if choose:
        state_specs = [
            pl.BlockSpec(state, lambda n, m: (held(m[0], m), 0, 0)),
            pl.BlockSpec(state, lambda n, m: (held(m[0] ^ 1, m), 0, 0)),
        ] + [pl.BlockSpec(state, lambda n, m: (0, 0, 0))] * (len(states) - 2)
    else:
        state_specs = [pl.BlockSpec((inner, STATE), whole)]
    out_specs = [
        pl.BlockSpec((count, share), whole)
        for q in range(shares)
    ] + [pl.BlockSpec((8, LANES), lambda n, m: (0, jnp.minimum(n, chunks - 1)))]
    out_shape = [jax.ShapeDtypeStruct((count, share), BF16)] * shares + [
        jax.ShapeDtypeStruct((8, count), F32)
    ]
    if choose:
        out_specs.append(pl.BlockSpec((inner, STATE), whole))
        out_shape.append(jax.ShapeDtypeStruct((inner, STATE), BF16))
    return pl.pallas_call(
        functools.partial(project_kernel, chunks, shares, (reqs, slots) if choose else None),
        grid_spec=pltpu.PrefetchScalarGridSpec(
            num_scalar_prefetch=1,
            grid=(chunks + shares,),
            in_specs=state_specs
            + [
                pl.BlockSpec((SPAN, inner), rows),
                pl.BlockSpec((SPAN, inner), rows),
                pl.BlockSpec((SPAN, LANES), rows),
                pl.BlockSpec((SPAN, LANES), rows),
                pl.BlockSpec((1, inner), whole),
                pl.BlockSpec((LANES, inner), whole),
                pl.BlockSpec(memory_space=pl.ANY),
            ],
            out_specs=out_specs,
            scratch_shapes=[
                pltpu.VMEM((count, inner), BF16),
                pltpu.VMEM((shares, inner, share), BF16),
                pltpu.SemaphoreType.DMA((shares,)),
            ],
        ),
        out_shape=out_shape,
        compiler_params=pltpu.CompilerParams(
            dimension_semantics=("arbitrary",), vmem_limit_bytes=36 * 2**20
        ),
        cost_estimate=pl.CostEstimate(
            flops=2 * count * inner * width,
            bytes_accessed=2 * inner * width + 10 * 2**20,
            transcendentals=count * inner,
        ),
        name="project",
    )(meta, *states, y, gate, cmap, reach, gain, pick, weight)


def line_sums(parts, mark, size):
    to_right = [(i, i + 1) for i in range(size - 1)]
    to_left = [(i + 1, i) for i in range(size - 1)]
    add = lambda a, b: (a.astype(F32) + b.astype(F32)).astype(BF16)
    right = [None] * len(parts)
    left = [None] * len(parts)
    for s in range(size - 1):
        for p in range(len(parts)):
            part = parts[p]
            go_right, go_left = part[size - 1 - s], part[s + 1]
            if s:
                go_right, go_left = add(go_right, right[p]), add(go_left, left[p])
            right[p] = lax.ppermute(go_right, "tp", to_right[: s + 1])
            left[p] = lax.ppermute(go_left, "tp", to_left[size - 2 - s :])
            if s == 0 and p + 1 < len(parts):
                right[p], left[p], parts[p + 1], mark = lax.optimization_barrier(
                    (right[p], left[p], parts[p + 1], mark)
                )
    return mark, [
        part[0].astype(F32) + r.astype(F32) + l.astype(F32)
        for part, r, l in zip(parts, right, left)
    ]


def source_of(meta, device, reqs):
    found = jnp.int32(0)
    for r in range(reqs):
        found += jnp.where(meta[2 + 2 * reqs + r] == device, r, 0)
    return found


def ending_kernel(reqs, meta, mark_ref, local_ref, start_ref, total_ref, pick_ref, conv_ref, x_ref, bc_ref, out_ref):
    inner = local_ref.shape[0]
    length = meta[2 + 3 * reqs + meta[0]]
    for i in range(inner // WIDE):
        at = pl.ds(i * WIDE, WIDE)
        decay = dot(total_ref[...], pick_ref[:, at])[0:1]
        decay = jnp.transpose(jnp.broadcast_to(decay, (STATE, WIDE)))
        out_ref[at, :] = (local_ref[at, :] + decay * start_ref[at, :].astype(F32)).astype(BF16)
    row = lax.broadcasted_iota(jnp.int32, (16, SUF), 0) + length - (CONV - 1)
    found = (row == lax.broadcasted_iota(jnp.int32, (16, SUF), 1)).astype(BF16)
    conv = conv_ref[...].astype(F32)
    row = lax.broadcasted_iota(jnp.int32, (16, WIDE), 0) + length
    for i in range((inner + BCW) // WIDE):
        at = i * WIDE
        source = x_ref[:, at : at + WIDE] if at < inner else bc_ref[:, at - inner : at - inner + WIDE]
        tail = dot(found, source)
        for k in range(CONV - 1):
            tail += jnp.where(row == k, conv[k : k + 1, at : at + WIDE], 0.0)
        tail = tail.astype(BF16)
        for j in range(WIDE // LANES):
            to = inner + (at // LANES + j) * 16
            out_ref[to : to + 16, :] = tail[:, j * LANES : (j + 1) * LANES]


def run_ending(meta, mark, local, start, total, pick, conv, x, bc, reqs):
    inner = local.shape[0]
    rows = inner + (inner + BCW) // LANES * 16
    operands = (mark, local, start, total, pick, conv, x, bc)
    return pl.pallas_call(
        functools.partial(ending_kernel, reqs),
        grid_spec=pltpu.PrefetchScalarGridSpec(
            num_scalar_prefetch=1,
            grid=(1,),
            in_specs=[pl.BlockSpec(a.shape, lambda i, m: (0, 0)) for a in operands],
            out_specs=pl.BlockSpec((rows, LANES), lambda i, m: (0, 0)),
        ),
        out_shape=jax.ShapeDtypeStruct((rows, LANES), BF16),
        compiler_params=pltpu.CompilerParams(vmem_limit_bytes=24 * 2**20),
        cost_estimate=pl.CostEstimate(flops=10**8, bytes_accessed=6 * 2**20, transcendentals=0),
        name="ending",
    )(meta, *operands)


def route_kernel(reqs, meta, *refs):
    origin = over(source_of(meta, meta[0] ^ 1, reqs), 2)
    away = wrap(over(meta[0], 2) - origin + reqs // 2, reqs // 2)
    taken = refs[0][...]
    for k in range(1, reqs // 2):
        taken = jnp.where(away == k, refs[k][...], taken)
    refs[-1][...] = taken


def run_route(meta, ends, reqs):
    shape = ends[0].shape
    return pl.pallas_call(
        functools.partial(route_kernel, reqs),
        grid_spec=pltpu.PrefetchScalarGridSpec(
            num_scalar_prefetch=1,
            grid=(1,),
            in_specs=[pl.BlockSpec(shape, lambda i, m: (0, 0))] * len(ends),
            out_specs=pl.BlockSpec(shape, lambda i, m: (0, 0)),
        ),
        out_shape=jax.ShapeDtypeStruct(shape, BF16),
        compiler_params=pltpu.CompilerParams(vmem_limit_bytes=12 * 2**20),
        cost_estimate=pl.CostEstimate(flops=10**6, bytes_accessed=2 * 2**20, transcendentals=0),
        name="route",
    )(meta, *ends)


def land_kernel(reqs, meta, *refs):
    state_ref, x_ref, bc_ref = refs[-3:]
    crossed_ref = refs[-4]
    source = source_of(meta, meta[0], reqs)
    away = wrap(over(meta[0], 2) - over(source, 2) + reqs // 2, reqs // 2)
    inner = state_ref.shape[0]

    def taken(at):
        value = refs[0][at, :]
        for k in range(1, reqs // 2):
            value = jnp.where(away == k, refs[k][at, :], value)
        return jnp.where((source & 1) == (meta[0] & 1), value, crossed_ref[at, :])

    for i in range(inner // WIDE):
        at = pl.ds(i * WIDE, WIDE)
        state_ref[at, :] = taken(at).astype(F32)
    tiles = (inner + BCW) // LANES
    tails = [taken(pl.ds(inner + j * 16, 16))[: CONV - 1] for j in range(tiles)]
    x_ref[...] = jnp.concatenate(tails[: inner // LANES], axis=1)
    bc_ref[...] = jnp.concatenate(tails[inner // LANES :], axis=1)


def run_land(meta, ends, crossed, inner, reqs):
    shape = crossed.shape
    outs = [(inner, STATE), (CONV - 1, inner), (CONV - 1, BCW)]
    return pl.pallas_call(
        functools.partial(land_kernel, reqs),
        grid_spec=pltpu.PrefetchScalarGridSpec(
            num_scalar_prefetch=1,
            grid=(1,),
            in_specs=[pl.BlockSpec(shape, lambda i, m: (0, 0))] * (len(ends) + 1),
            out_specs=[pl.BlockSpec(o, lambda i, m: (0, 0)) for o in outs],
        ),
        out_shape=[jax.ShapeDtypeStruct(o, t) for o, t in zip(outs, (F32, BF16, BF16))],
        compiler_params=pltpu.CompilerParams(vmem_limit_bytes=16 * 2**20),
        cost_estimate=pl.CostEstimate(flops=10**6, bytes_accessed=3 * 2**20, transcendentals=0),
        name="land",
    )(meta, *ends, crossed)


def shifted(x, axis, size, by):
    return lax.ppermute(x, axis, [(i, (i + by) % size) for i in range(size)])


def swap_core(x, size):
    return lax.ppermute(x, "req", [(i, i ^ 1) for i in range(size)])


def per_device(
    ssm_input,
    gate_input,
    bc_input,
    dt_input,
    decay_rate,
    skip_gain,
    norm_gain,
    conv_x_weight,
    conv_bc_weight,
    out_weight,
    pool_states,
    pool_conv_x,
    pool_conv_bc,
    prefix_slot,
    prefix_spans,
    dest_slot,
    suffix_len,
):
    num_req = lax.axis_size("req")
    num_tp = lax.axis_size("tp")
    me = lax.axis_index("req")
    z = lax.axis_index("tp")
    heads = dt_input.shape[1]
    inner = ssm_input.shape[1]
    slots = pool_states.shape[0]
    meta = jnp.concatenate(
        [jnp.stack([me, z]), prefix_slot, prefix_spans, dest_slot, suffix_len]
    ).astype(jnp.int32)

    mine = pool_states.reshape(slots, inner, STATE)
    other = swap_core(mine, num_req)
    conv = run_pack(
        meta,
        jnp.transpose(pool_conv_x, (1, 0, 2)),
        jnp.transpose(pool_conv_bc, (1, 0, 2)),
        num_req,
    )
    convs = [conv[0]] + [shifted(conv[by], "req", num_req, by) for by in range(1, num_req)]
    chosen, mark = run_choose(meta, mine, other, num_req)
    got = [
        shifted(chosen[k : k + 1], "req", num_req, 2 * k + 2) for k in range(num_req // 2 - 1)
    ]

    y_local, local_final, cmap, reach, total, start_conv, pick = run_scan(
        meta,
        convs,
        mark,
        ssm_input,
        bc_input,
        dt_input.T,
        decay_rate,
        skip_gain,
        conv_x_weight,
        conv_bc_weight,
        heads,
        slots,
    )
    states = [mine, other] + got
    parts, squares = [], []
    first = 0
    for chunks in PIECES:
        result = run_project(
            first,
            chunks,
            meta,
            states,
            y_local,
            gate_input,
            cmap,
            reach,
            norm_gain[None, :],
            pick,
            out_weight,
            num_tp,
            num_req,
        )
        first += chunks
        parts.append(tuple(result[:num_tp]))
        squares.append(result[num_tp][0])
        if len(states) > 1:
            start = result[num_tp + 1]
            states = [start]
    mark, summed = line_sums(parts, result[num_tp], num_tp)
    summed = jnp.concatenate(summed, axis=0)

    my_len = suffix_len[me]
    square = jnp.concatenate(squares)
    square_total = square
    for by in range(1, num_tp):
        square_total = square_total + shifted(square, "tp", num_tp, by)
    scale = lax.rsqrt(square_total / INNER + 1e-05)
    scale = jnp.where(jnp.arange(SUF) < my_len, scale, 0.0)
    mixed = (summed * scale[:, None]).astype(BF16)

    end = run_ending(
        meta, mark, local_final, start, total, pick, start_conv, ssm_input, bc_input, num_req
    )
    ends = [end] + [shifted(end, "req", num_req, by) for by in range(2, num_req, 2)]
    crossed = swap_core(run_route(meta, ends, num_req), num_req)
    ckpt_states, ckpt_x, ckpt_bc = run_land(meta, ends, crossed, inner, num_req)
    return (
        mixed,
        ckpt_states.reshape((1, heads, HDIM, STATE)),
        ckpt_x[None],
        ckpt_bc[None],
    )


def solution(mesh):
    return jax.shard_map(
        per_device,
        mesh=mesh,
        in_specs=(
            P(("groups", "req"), "tp"),
            P(("groups", "req"), "tp"),
            P(("groups", "req"), None),
            P(("groups", "req"), "tp"),
            P("tp"),
            P("tp"),
            P("tp"),
            P(None, "tp"),
            P(),
            P("tp", None),
            P(("groups", "req"), "tp", None, None),
            P(("groups", "req"), None, "tp"),
            P(("groups", "req"), None, None),
            P("groups"),
            P("groups"),
            P("groups"),
            P("groups"),
        ),
        out_specs=(
            P(("groups", "req"), "tp"),
            P(("groups", "req"), "tp", None, None),
            P(("groups", "req"), None, "tp"),
            P(("groups", "req"), None, None),
        ),
        check_vma=False,
    )
```

```python
import functools

import jax
import jax.numpy as jnp
from jax import lax
from jax.experimental import pallas as pl
from jax.experimental.pallas import tpu as pltpu
from jax.sharding import PartitionSpec as P

HDIM = 64
STATE = 128
GHEADS = 32
CONV = 4
SPAN = 128
SUF = 512
INNER = 8192
BCG = 4
BCW = 1024
NCH = 4
LANES = 128
WIDE = 512
PIECE = 2
PROJ = 36
AHEAD = 3

F32 = jnp.float32
BF16 = jnp.bfloat16
HIGH = lax.Precision.HIGHEST


def wrap(x, n):
    return x & (n - 1) if n & (n - 1) == 0 else x % n


def over(x, n):
    return x >> (n.bit_length() - 1) if n & (n - 1) == 0 else x // n


def silu(x):
    half = 0.5 * x
    return half + half * jnp.tanh(half)


def split_pair(x, heads):
    lane = lax.broadcasted_iota(jnp.int32, x.shape, 1)
    high = x.astype(BF16).astype(F32)
    rest = jnp.where(lane < 2 * heads, x - high, 0.0)
    return jnp.where(lane < heads, high, rest).astype(BF16)


def dot(a, b):
    return jnp.dot(a, b, preferred_element_type=F32)


def dot_t(a, b):
    return lax.dot_general(a, b, (((1,), (1,)), ((), ())), preferred_element_type=F32)


def conv_taps(before, x, weight):
    extended = jnp.concatenate([before, x], axis=0)
    total = extended[8:] * weight[CONV - 1 :]
    for k in range(CONV - 1):
        total += extended[5 + k : 5 + k + SPAN] * weight[k : k + 1]
    return total


def pack_kernel(reqs, meta, px_ref, pb_ref, *conv_refs):
    slots = px_ref.shape[1]
    inner = px_ref.shape[2]
    me = meta[0]
    px = px_ref[...].astype(F32)
    pb = pb_ref[...].astype(F32)
    for by in range(reqs):
        at = jnp.clip(meta[2 + wrap(me + by, reqs)] - slots * me, 0, slots - 1)
        sent_x, sent_b = px[:, 0], pb[:, 0]
        for s in range(1, slots):
            sent_x = jnp.where(at == s, px[:, s], sent_x)
            sent_b = jnp.where(at == s, pb[:, s], sent_b)
        conv_refs[by][:, :inner] = sent_x.astype(BF16)
        conv_refs[by][:, inner:] = sent_b.astype(BF16)


def run_pack(meta, px, pb, reqs):
    taps, _, inner = px.shape
    return pl.pallas_call(
        functools.partial(pack_kernel, reqs),
        grid_spec=pltpu.PrefetchScalarGridSpec(
            num_scalar_prefetch=1,
            grid=(1,),
            in_specs=[
                pl.BlockSpec(px.shape, lambda i, m: (0, 0, 0)),
                pl.BlockSpec(pb.shape, lambda i, m: (0, 0, 0)),
            ],
            out_specs=[pl.BlockSpec((taps, inner + BCW), lambda i, m: (0, 0))] * reqs,
        ),
        out_shape=[jax.ShapeDtypeStruct((taps, inner + BCW), BF16)] * reqs,
        compiler_params=pltpu.CompilerParams(vmem_limit_bytes=8 * 2**20),
        cost_estimate=pl.CostEstimate(flops=10**6, bytes_accessed=2**18, transcendentals=0),
        name="pack",
    )(meta, px, pb)


def choose_kernel(reqs, slots, meta, mine_ref, mate_ref, out_ref, mark_ref):
    slot = meta[2 + wrap(meta[0] + 2 + 2 * pl.program_id(0), reqs)]
    out_ref[...] = jnp.where(over(slot, slots) == meta[0], mine_ref[...], mate_ref[...]).astype(BF16)
    mark_ref[...] = jnp.zeros_like(mark_ref)


def run_choose(meta, mine, mate, reqs):
    slots, inner, _ = mine.shape
    shape = (1, WIDE, STATE)

    def held(meta, by, owner):
        return jnp.clip(meta[2 + wrap(meta[0] + 2 + 2 * by, reqs)] - slots * owner, 0, slots - 1)

    return pl.pallas_call(
        functools.partial(choose_kernel, reqs, slots),
        grid_spec=pltpu.PrefetchScalarGridSpec(
            num_scalar_prefetch=1,
            grid=(reqs // 2 - 1, inner // WIDE),
            in_specs=[
                pl.BlockSpec(shape, lambda i, j, m: (held(m, i, m[0]), j, 0)),
                pl.BlockSpec(shape, lambda i, j, m: (held(m, i, m[0] ^ 1), j, 0)),
            ],
            out_specs=[
                pl.BlockSpec(shape, lambda i, j, m: (i, j, 0)),
                pl.BlockSpec((8, LANES), lambda i, j, m: (0, 0)),
            ],
        ),
        out_shape=[
            jax.ShapeDtypeStruct((reqs // 2 - 1, inner, STATE), BF16),
            jax.ShapeDtypeStruct((8, LANES), F32),
        ],
        compiler_params=pltpu.CompilerParams(vmem_limit_bytes=8 * 2**20),
        cost_estimate=pl.CostEstimate(flops=10**6, bytes_accessed=2 * 2**20, transcendentals=0),
        name="choose",
    )(meta, mine, mate)


def scan_kernel(
    heads,
    slots,
    reqs,
    meta,
    *refs,
):
    scan_body(heads, slots, reqs, meta, refs[:reqs], *refs[reqs + 1 :])


def scan_body(
    heads,
    slots,
    reqs,
    meta,
    conv_refs,
    x_ref,
    b_ref,
    c_ref,
    dt_ref,
    rate_ref,
    skip_ref,
    wx_ref,
    wb_ref,
    wc_ref,
    y_ref,
    final_ref,
    cmap_ref,
    reach_ref,
    total_ref,
    conv_ref,
    pick_ref,
    start,
    state,
    tail_x,
    tail_m,
    left,
    bmap_t,
    factors,
    base,
):
    block = pl.program_id(0)
    c = pl.program_id(1)
    me = meta[0]
    slot = meta[2 + me]
    inner = conv_ref.shape[1] - BCW
    wide = x_ref.shape[1]
    group = over(meta[1] * heads, GHEADS)

    @pl.when((block == 0) & (c == 0))
    def _():
        away = wrap(me - over(slot, slots) + reqs, reqs)
        taken = conv_refs[0][...].astype(F32)
        for by in range(1, reqs):
            taken = jnp.where(away == by, conv_refs[by][...].astype(F32), taken)
        taken = jnp.where(meta[2 + reqs + me] > 0, taken, 0.0)
        start[...] = jnp.concatenate(
            [jnp.zeros((8 - (CONV - 1), inner + BCW), F32), taken], axis=0
        )
        conv_ref[...] = taken.astype(BF16)

    @pl.when(block == 0)
    def _():
        maps = []
        for k, (ref, w) in enumerate(((b_ref, wb_ref), (c_ref, wc_ref))):
            at = pl.multiple_of(inner + (group + k * BCG) * LANES, LANES)
            before = jnp.where(c == 0, start[:, pl.ds(at, LANES)], tail_m[k])
            x = ref[...].astype(F32)
            maps.append(silu(conv_taps(before, x, w[...].astype(F32))).astype(BF16))
            tail_m[k] = x[SPAN - 8 :]
        bmap, cmap = maps
        row = lax.broadcasted_iota(jnp.int32, (SPAN, SPAN), 0)
        col = lax.broadcasted_iota(jnp.int32, (SPAN, SPAN), 1)
        scores = jnp.where(row >= col, dot_t(cmap, bmap), 0.0).astype(BF16)
        left[c, :, :SPAN] = scores
        left[c, :, SPAN:] = cmap
        cmap_ref[...] = cmap
        bmap_t[c] = jnp.transpose(bmap.astype(F32)).astype(BF16)

        @pl.when(c == 0)
        def _():
            base[...] = jnp.zeros_like(base)

        copies = LANES // heads
        logit = jnp.transpose(jnp.concatenate([dt_ref[...]] * copies, axis=0))
        rate = jnp.concatenate([rate_ref[...].reshape(1, heads)] * copies, axis=1)
        skip = jnp.concatenate([skip_ref[...].reshape(1, heads)] * copies, axis=1)
        live = (row + c * SPAN < meta[2 + 3 * reqs + me]).astype(F32)
        step = (jnp.maximum(logit, 0.0) + jnp.log1p(jnp.exp(-jnp.abs(logit)))) * live
        cum = jnp.dot(
            (row >= col).astype(F32),
            -step * rate,
            precision=HIGH,
            preferred_element_type=F32,
        )
        last = cum[SPAN - 1 :]
        mid = 0.5 * last
        factors[c, :SPAN] = split_pair(jnp.exp(cum - mid), heads)
        factors[c, SPAN : 2 * SPAN] = split_pair(jnp.exp(mid - cum) * step, heads)
        before = base[0:1]
        reach_ref[...] = split_pair(jnp.exp(before + cum), heads)
        which = lax.broadcasted_iota(jnp.int32, (16, LANES), 0)
        singles = jnp.where(which == 1, jnp.exp(last - mid), skip)
        factors[c, 2 * SPAN :] = split_pair(jnp.where(which == 0, jnp.exp(mid), singles), heads)
        base[...] = base[...] + last
        total_ref[...] = split_pair(jnp.exp(base[...]), heads)

    @pl.when(c == 0)
    def _():
        state[...] = jnp.zeros_like(state)
        lane = lax.broadcasted_iota(jnp.int32, (LANES, wide), 0)
        channel = lax.broadcasted_iota(jnp.int32, (LANES, wide), 1) + block * wide
        pick_ref[...] = ((wrap(lane, heads) == over(channel, HDIM)) & (lane < 2 * heads)).astype(BF16)
        tail_x[...] = start[:, pl.ds(pl.multiple_of(block * wide, wide), wide)]

    x = x_ref[...].astype(F32)
    conv = conv_taps(tail_x[...], x, wx_ref[...].astype(F32))
    tail_x[...] = x[SPAN - 8 :]
    values = silu(conv).astype(BF16).astype(F32)
    spread = dot(factors[c], pick_ref[...])
    rows = spread[2 * SPAN :]
    scaled = (values * spread[SPAN : 2 * SPAN]).astype(BF16)
    held = state[...] * rows[0:1]
    right = jnp.concatenate([scaled, held.astype(BF16)], axis=0)
    y_ref[...] = (dot(left[c], right) * spread[:SPAN] + rows[2:3] * values).astype(BF16)
    state[...] = (held + dot(bmap_t[c], scaled)) * rows[1:2]

    @pl.when(c == NCH - 1)
    def _():
        final_ref[...] = jnp.transpose(state[...]).astype(BF16)


def run_scan(meta, conv, mark, x, bc, dt, rate, skip, wx, wbc, heads, slots):
    inner = x.shape[1]
    wide = min(2048, inner)
    blocks = inner // wide
    reqs = len(conv)
    once = lambda b, c: jnp.where(b == 0, c, NCH - 1)
    group = lambda m: over(m[1] * heads, GHEADS)
    in_specs = [pl.BlockSpec((CONV - 1, inner + BCW), lambda b, c, m: (0, 0))] * reqs
    in_specs += [
        pl.BlockSpec((8, LANES), lambda b, c, m: (0, 0)),
        pl.BlockSpec((SPAN, wide), lambda b, c, m: (c, b)),
        pl.BlockSpec((SPAN, LANES), lambda b, c, m: (once(b, c), group(m))),
        pl.BlockSpec((SPAN, LANES), lambda b, c, m: (once(b, c), group(m) + BCG)),
        pl.BlockSpec((heads, SPAN), lambda b, c, m: (0, once(b, c))),
        pl.BlockSpec((heads,), lambda b, c, m: (0,)),
        pl.BlockSpec((heads,), lambda b, c, m: (0,)),
        pl.BlockSpec((CONV, wide), lambda b, c, m: (0, b)),
        pl.BlockSpec((CONV, LANES), lambda b, c, m: (0, group(m))),
        pl.BlockSpec((CONV, LANES), lambda b, c, m: (0, group(m) + BCG)),
    ]
    out_specs = [
        pl.BlockSpec((SPAN, wide), lambda b, c, m: (c, b)),
        pl.BlockSpec((wide, STATE), lambda b, c, m: (b, 0)),
        pl.BlockSpec((SPAN, LANES), lambda b, c, m: (once(b, c), 0)),
        pl.BlockSpec((SPAN, LANES), lambda b, c, m: (once(b, c), 0)),
        pl.BlockSpec((16, LANES), lambda b, c, m: (0, 0)),
        pl.BlockSpec((CONV - 1, inner + BCW), lambda b, c, m: (0, 0)),
        pl.BlockSpec((LANES, wide), lambda b, c, m: (0, b)),
    ]
    return pl.pallas_call(
        functools.partial(scan_kernel, heads, slots, reqs),
        grid_spec=pltpu.PrefetchScalarGridSpec(
            num_scalar_prefetch=1,
            grid=(blocks, NCH),
            in_specs=in_specs,
            out_specs=out_specs,
            scratch_shapes=[
                pltpu.VMEM((8, inner + BCW), F32),
                pltpu.VMEM((STATE, wide), F32),
                pltpu.VMEM((8, wide), F32),
                pltpu.VMEM((2, 8, LANES), F32),
                pltpu.VMEM((NCH, SPAN, 2 * SPAN), BF16),
                pltpu.VMEM((NCH, STATE, SPAN), BF16),
                pltpu.VMEM((NCH, 2 * SPAN + 16, LANES), BF16),
                pltpu.VMEM((16, LANES), F32),
            ],
        ),
        out_shape=[
            jax.ShapeDtypeStruct((SUF, inner), BF16),
            jax.ShapeDtypeStruct((inner, STATE), BF16),
            jax.ShapeDtypeStruct((SUF, LANES), BF16),
            jax.ShapeDtypeStruct((SUF, LANES), BF16),
            jax.ShapeDtypeStruct((16, LANES), BF16),
            jax.ShapeDtypeStruct((CONV - 1, inner + BCW), BF16),
            jax.ShapeDtypeStruct((LANES, inner), BF16),
        ],
        compiler_params=pltpu.CompilerParams(
            dimension_semantics=("arbitrary", "arbitrary"), vmem_limit_bytes=16 * 2**20
        ),
        cost_estimate=pl.CostEstimate(
            flops=8 * 10**9, bytes_accessed=12 * 2**20, transcendentals=SUF * inner
        ),
        name="local_scan",
    )(meta, *conv, mark, x, bc, bc, dt, rate, skip, wx, wbc, wbc)


def project_kernel(chunks, shares, picks, emit, late, meta, *refs):
    if picks:
        reqs, slots = picks
        others = reqs // 2 - 1
        mine_ref, mate_ref = refs[:2]
        got_refs = refs[2 : 2 + others]
        refs = refs[2 + others :]
    else:
        start_ref, refs = refs[0], refs[1:]
    if late:
        before_ref, refs = refs[0], refs[1:]
    y_ref, gate_ref, cmap_ref, reach_ref, gain_ref, pick_ref, w_ref = refs[:7]
    out_refs = refs[7 : 7 + len(emit)]
    late_refs = refs[7 + len(emit) : 7 + len(emit) + len(late)]
    refs = refs[7 + len(emit) + len(late) :]
    sq_ref = refs[0]
    if picks:
        start_ref = refs[1]
    held, w_held, arrived = refs[-3:]
    step = pl.program_id(0)
    inner = y_ref.shape[1]
    share = out_refs[0].shape[1]

    def fetch(i):
        q = emit[i]
        to = jnp.where(2 * meta[1] < shares, meta[1] + q, meta[1] - q + shares)
        column = pl.multiple_of(wrap(to, shares) * share, share)
        return pltpu.make_async_copy(
            w_ref.at[:, pl.ds(column, share)], w_held.at[i % AHEAD], arrived.at[i % AHEAD]
        )

    @pl.when(step == 0)
    def _():
        for i in range(min(AHEAD, len(emit))):
            fetch(i).start()

    if picks:

        @pl.when(step == 0)
        def _():
            me = meta[0]
            owner = over(meta[2 + me], slots)
            away = wrap(over(me, 2) - over(owner, 2) + reqs // 2, reqs // 2)
            taken = jnp.where(owner == me, mine_ref[0], mate_ref[0])
            for k in range(others):
                taken = jnp.where(away == k + 1, got_refs[k][0].astype(F32), taken)
            start_ref[...] = jnp.where(meta[2 + reqs + me] > 0, taken, 0.0).astype(BF16)

    @pl.when(step < chunks)
    def _():
        squares = jnp.zeros((SPAN, LANES), F32)
        rows = pl.ds(pl.multiple_of(step * SPAN, SPAN), SPAN)
        for i in range(inner // WIDE):
            at = pl.ds(i * WIDE, WIDE)
            carried = dot_t(cmap_ref[...], start_ref[at, :])
            y = y_ref[:, at].astype(F32) + dot(reach_ref[...], pick_ref[:, at]) * carried
            gated = y * silu(gate_ref[:, at].astype(F32))
            held[rows, at] = (gated * gain_ref[:, at]).astype(BF16)
            gated = gated * gated
            for j in range(WIDE // LANES):
                squares += gated[:, j * LANES : (j + 1) * LANES]
        sq_ref[...] = lax.dot_general(
            jnp.ones((8, LANES), F32),
            squares,
            (((1,), (1,)), ((), ())),
            precision=HIGH,
            preferred_element_type=F32,
        )

    for i in range(len(emit)):

        @pl.when(step == chunks + i)
        def _(i=i):
            fetch(i).wait()
            out_refs[i][...] = dot(held[...], w_held[i % AHEAD]).astype(BF16)
            if emit[i] in late:
                late_refs[late.index(emit[i])][...] = dot(
                    before_ref[...], w_held[i % AHEAD]
                ).astype(BF16)
            if i + AHEAD < len(emit):
                fetch(i + AHEAD).start()


def run_project(
    first, chunks, emit, late, meta, states, before, y, gate, cmap, reach, gain, pick, weight, shares, reqs
):
    inner, width = weight.shape
    share = width // shares
    count = chunks * SPAN
    rows = lambda n, m: (first + jnp.minimum(n, chunks - 1), 0)
    whole = lambda n, m: (0, 0)
    state = (1, inner, STATE)
    choose = len(states) > 1
    single = pl.Buffered(1)
    slots = states[0].shape[0]

    def held(owner, m):
        return jnp.clip(m[2 + m[0]] - slots * owner, 0, slots - 1)

    if choose:
        state_specs = [
            pl.BlockSpec(state, lambda n, m: (held(m[0], m), 0, 0), pipeline_mode=single),
            pl.BlockSpec(state, lambda n, m: (held(m[0] ^ 1, m), 0, 0), pipeline_mode=single),
        ] + [pl.BlockSpec(state, lambda n, m: (0, 0, 0), pipeline_mode=single)] * (len(states) - 2)
    else:
        state_specs = [pl.BlockSpec((inner, STATE), whole, pipeline_mode=single)]
    out_specs = [
        pl.BlockSpec((count, share), whole)
        for q in emit
    ]
    out_specs += [pl.BlockSpec((first * SPAN, share), whole) for q in late]
    out_specs += [pl.BlockSpec((8, LANES), lambda n, m: (0, jnp.minimum(n, chunks - 1)))]
    out_shape = [jax.ShapeDtypeStruct((count, share), BF16)] * len(emit)
    out_shape += [jax.ShapeDtypeStruct((first * SPAN, share), BF16)] * len(late)
    out_shape.append(jax.ShapeDtypeStruct((8, count), F32))
    if choose:
        out_specs.append(pl.BlockSpec((inner, STATE), whole))
        out_shape.append(jax.ShapeDtypeStruct((inner, STATE), BF16))
    gated = jax.ShapeDtypeStruct((count, inner), BF16)
    scratch = []
    if late:
        state_specs.append(pl.BlockSpec(before[0].shape, whole, pipeline_mode=single))
        scratch.append(pltpu.VMEM(gated.shape, BF16))
    else:
        out_specs.append(pl.BlockSpec(gated.shape, whole))
        out_shape.append(gated)
    return pl.pallas_call(
        functools.partial(project_kernel, chunks, shares, (reqs, slots) if choose else None, emit, late),
        grid_spec=pltpu.PrefetchScalarGridSpec(
            num_scalar_prefetch=1,
            grid=(chunks + len(emit),),
            in_specs=state_specs
            + [
                pl.BlockSpec((SPAN, inner), rows),
                pl.BlockSpec((SPAN, inner), rows),
                pl.BlockSpec((SPAN, LANES), rows),
                pl.BlockSpec((SPAN, LANES), rows),
                pl.BlockSpec((1, inner), whole),
                pl.BlockSpec((LANES, inner), whole, pipeline_mode=single),
                pl.BlockSpec(memory_space=pl.ANY),
            ],
            out_specs=out_specs,
            scratch_shapes=scratch
            + [
                pltpu.VMEM((AHEAD, inner, share), BF16),
                pltpu.SemaphoreType.DMA((AHEAD,)),
            ],
        ),
        out_shape=out_shape,
        compiler_params=pltpu.CompilerParams(
            dimension_semantics=("arbitrary",), vmem_limit_bytes=PROJ * 2**20
        ),
        cost_estimate=pl.CostEstimate(flops=1, bytes_accessed=1, transcendentals=0),
        name="project",
    )(meta, *states, *before, y, gate, cmap, reach, gain, pick, weight)


def line_sums(parts, mark, size):
    parts = list(parts)
    sums = []
    for p in range(len(parts)):
        landed = []
        came = {}
        for k in range(size - 1):
            for d in range(size - 1, k, -1):
                slot = d - k if 2 * k < size else size - d + k
                go = parts[p][slot]
                if k:
                    go = (go.astype(F32) + came[k - 1, d].astype(F32)).astype(BF16)
                came[k, d] = lax.ppermute(
                    go, "tp", [(k, k + 1), (size - 1 - k, size - 2 - k)]
                )
                if k == 0 and d == size - 1 and p + 1 < len(parts):
                    came[k, d], parts[p + 1], mark = lax.optimization_barrier(
                        (came[k, d], parts[p + 1], mark)
                    )
            landed.append(came[k, k + 1])
        total = parts[p][0].astype(F32)
        for value in landed:
            total += value.astype(F32)
        sums.append(total)
    return mark, sums


def source_of(meta, device, reqs):
    found = jnp.int32(0)
    for r in range(reqs):
        found += jnp.where(meta[2 + 2 * reqs + r] == device, r, 0)
    return found


def ending_kernel(reqs, meta, mark_ref, local_ref, start_ref, total_ref, pick_ref, conv_ref, x_ref, bc_ref, out_ref):
    inner = local_ref.shape[0]
    length = meta[2 + 3 * reqs + meta[0]]
    for i in range(inner // WIDE):
        at = pl.ds(i * WIDE, WIDE)
        decay = dot(total_ref[...], pick_ref[:, at])[0:1]
        decay = jnp.transpose(jnp.broadcast_to(decay, (STATE, WIDE)))
        out_ref[at, :] = (local_ref[at, :].astype(F32) + decay * start_ref[at, :].astype(F32)).astype(BF16)
    row = lax.broadcasted_iota(jnp.int32, (16, SUF), 0) + length - (CONV - 1)
    found = (row == lax.broadcasted_iota(jnp.int32, (16, SUF), 1)).astype(BF16)
    conv = conv_ref[...].astype(F32)
    row = lax.broadcasted_iota(jnp.int32, (16, WIDE), 0) + length
    for i in range((inner + BCW) // WIDE):
        at = i * WIDE
        source = x_ref[:, at : at + WIDE] if at < inner else bc_ref[:, at - inner : at - inner + WIDE]
        tail = dot(found, source)
        for k in range(CONV - 1):
            tail += jnp.where(row == k, conv[k : k + 1, at : at + WIDE], 0.0)
        tail = tail.astype(BF16)
        for j in range(WIDE // LANES):
            to = inner + (at // LANES + j) * 16
            out_ref[to : to + 16, :] = tail[:, j * LANES : (j + 1) * LANES]


def run_ending(meta, mark, local, start, total, pick, conv, x, bc, reqs):
    inner = local.shape[0]
    rows = inner + (inner + BCW) // LANES * 16
    operands = (mark, local, start, total, pick, conv, x, bc)
    return pl.pallas_call(
        functools.partial(ending_kernel, reqs),
        grid_spec=pltpu.PrefetchScalarGridSpec(
            num_scalar_prefetch=1,
            grid=(1,),
            in_specs=[pl.BlockSpec(a.shape, lambda i, m: (0, 0)) for a in operands],
            out_specs=pl.BlockSpec((rows, LANES), lambda i, m: (0, 0)),
        ),
        out_shape=jax.ShapeDtypeStruct((rows, LANES), BF16),
        compiler_params=pltpu.CompilerParams(vmem_limit_bytes=16 * 2**20),
        cost_estimate=pl.CostEstimate(flops=1, bytes_accessed=1, transcendentals=0),
        name="ending",
    )(meta, *operands)


def route_kernel(reqs, meta, *refs):
    origin = over(source_of(meta, meta[0] ^ 1, reqs), 2)
    away = wrap(over(meta[0], 2) - origin + reqs // 2, reqs // 2)
    taken = refs[0][...]
    for k in range(1, reqs // 2):
        taken = jnp.where(away == k, refs[k][...], taken)
    refs[-1][...] = taken


def run_route(meta, ends, reqs):
    shape = ends[0].shape
    return pl.pallas_call(
        functools.partial(route_kernel, reqs),
        grid_spec=pltpu.PrefetchScalarGridSpec(
            num_scalar_prefetch=1,
            grid=(1,),
            in_specs=[pl.BlockSpec(shape, lambda i, m: (0, 0))] * len(ends),
            out_specs=pl.BlockSpec(shape, lambda i, m: (0, 0)),
        ),
        out_shape=jax.ShapeDtypeStruct(shape, BF16),
        compiler_params=pltpu.CompilerParams(vmem_limit_bytes=12 * 2**20),
        cost_estimate=pl.CostEstimate(flops=1, bytes_accessed=1, transcendentals=0),
        name="route",
    )(meta, *ends)


def land_kernel(reqs, meta, *refs):
    state_ref, x_ref, bc_ref = refs[-3:]
    crossed_ref = refs[-4]
    source = source_of(meta, meta[0], reqs)
    away = wrap(over(meta[0], 2) - over(source, 2) + reqs // 2, reqs // 2)
    inner = state_ref.shape[0]

    def taken(at):
        value = refs[0][at, :]
        for k in range(1, reqs // 2):
            value = jnp.where(away == k, refs[k][at, :], value)
        return jnp.where((source & 1) == (meta[0] & 1), value, crossed_ref[at, :])

    for i in range(inner // WIDE):
        at = pl.ds(i * WIDE, WIDE)
        state_ref[at, :] = taken(at).astype(F32)
    tiles = (inner + BCW) // LANES
    tails = [taken(pl.ds(inner + j * 16, 16))[: CONV - 1] for j in range(tiles)]
    x_ref[...] = jnp.concatenate(tails[: inner // LANES], axis=1)
    bc_ref[...] = jnp.concatenate(tails[inner // LANES :], axis=1)


def run_land(meta, ends, crossed, inner, reqs):
    shape = crossed.shape
    outs = [(inner, STATE), (CONV - 1, inner), (CONV - 1, BCW)]
    return pl.pallas_call(
        functools.partial(land_kernel, reqs),
        grid_spec=pltpu.PrefetchScalarGridSpec(
            num_scalar_prefetch=1,
            grid=(1,),
            in_specs=[pl.BlockSpec(shape, lambda i, m: (0, 0))] * (len(ends) + 1),
            out_specs=[pl.BlockSpec(o, lambda i, m: (0, 0)) for o in outs],
        ),
        out_shape=[jax.ShapeDtypeStruct(o, t) for o, t in zip(outs, (F32, BF16, BF16))],
        compiler_params=pltpu.CompilerParams(vmem_limit_bytes=16 * 2**20),
        cost_estimate=pl.CostEstimate(flops=1, bytes_accessed=1, transcendentals=0),
        name="land",
    )(meta, *ends, crossed)


def shifted(x, axis, size, by):
    return lax.ppermute(x, axis, [(i, (i + by) % size) for i in range(size)])


def swap_core(x, size):
    return lax.ppermute(x, "req", [(i, i ^ 1) for i in range(size)])


def per_device(
    ssm_input,
    gate_input,
    bc_input,
    dt_input,
    decay_rate,
    skip_gain,
    norm_gain,
    conv_x_weight,
    conv_bc_weight,
    out_weight,
    pool_states,
    pool_conv_x,
    pool_conv_bc,
    prefix_slot,
    prefix_spans,
    dest_slot,
    suffix_len,
):
    num_req = lax.axis_size("req")
    num_tp = lax.axis_size("tp")
    me = lax.axis_index("req")
    z = lax.axis_index("tp")
    heads = dt_input.shape[1]
    inner = ssm_input.shape[1]
    slots = pool_states.shape[0]
    meta = jnp.concatenate(
        [jnp.stack([me, z]), prefix_slot, prefix_spans, dest_slot, suffix_len]
    ).astype(jnp.int32)

    mine = pool_states.reshape(slots, inner, STATE)
    other = swap_core(mine, num_req)
    conv = run_pack(
        meta,
        jnp.transpose(pool_conv_x, (1, 0, 2)),
        jnp.transpose(pool_conv_bc, (1, 0, 2)),
        num_req,
    )
    chosen, mark = run_choose(meta, mine, other, num_req)
    conv, mark = lax.optimization_barrier((conv, mark))
    convs = [conv[0]] + [shifted(conv[by], "req", num_req, by) for by in range(1, num_req)]
    got = [
        shifted(chosen[k : k + 1], "req", num_req, 2 * k + 2) for k in range(num_req // 2 - 1)
    ]

    y_local, local_final, cmap, reach, total, start_conv, pick = run_scan(
        meta,
        convs,
        mark,
        ssm_input,
        bc_input,
        dt_input.T,
        decay_rate,
        skip_gain,
        conv_x_weight,
        conv_bc_weight,
        heads,
        slots,
    )
    states = [mine, other] + got
    operands = (y_local, gate_input, cmap, reach, norm_gain[None, :], pick, out_weight, num_tp, num_req)
    soon, rest = (num_tp - 1, num_tp - 2), tuple(range(num_tp - 2))
    first = run_project(0, PIECE, soon, (), meta, [mine, other] + got, [], *operands)
    start, gated = first[3], first[4]
    second = list(
        run_project(PIECE, NCH - PIECE, rest + soon, rest, meta, [start], [gated], *operands)
    )
    parts = [second[num_tp : num_tp + len(rest)] + [first[1], first[0]], list(second[: len(rest)])]
    parts[1] += [second[num_tp - 1], second[num_tp - 2]]
    parts = [tuple(part) for part in parts]
    result = {num_tp: second[-1]}
    squares = [first[2][0], second[-1][0]]
    mark, summed = line_sums(parts, result[num_tp], num_tp)
    summed = jnp.concatenate(summed, axis=0)

    my_len = suffix_len[me]
    square = jnp.concatenate(squares)
    square_total = square
    for by in range(1, num_tp):
        square_total = square_total + shifted(square, "tp", num_tp, by)
    scale = lax.rsqrt(square_total / INNER + 1e-05)
    scale = jnp.where(jnp.arange(SUF) < my_len, scale, 0.0)
    mixed = (summed * scale[:, None]).astype(BF16)

    end = run_ending(
        meta, mark, local_final, start, total, pick, start_conv, ssm_input, bc_input, num_req
    )
    ends = [end] + [shifted(end, "req", num_req, by) for by in range(2, num_req, 2)]
    crossed = swap_core(run_route(meta, ends, num_req), num_req)
    ckpt_states, ckpt_x, ckpt_bc = run_land(meta, ends, crossed, inner, num_req)
    return (
        mixed,
        ckpt_states.reshape((1, heads, HDIM, STATE)),
        ckpt_x[None],
        ckpt_bc[None],
    )


def solution(mesh):
    return jax.shard_map(
        per_device,
        mesh=mesh,
        in_specs=(
            P(("groups", "req"), "tp"),
            P(("groups", "req"), "tp"),
            P(("groups", "req"), None),
            P(("groups", "req"), "tp"),
            P("tp"),
            P("tp"),
            P("tp"),
            P(None, "tp"),
            P(),
            P("tp", None),
            P(("groups", "req"), "tp", None, None),
            P(("groups", "req"), None, "tp"),
            P(("groups", "req"), None, None),
            P("groups"),
            P("groups"),
            P("groups"),
            P("groups"),
        ),
        out_specs=(
            P(("groups", "req"), "tp"),
            P(("groups", "req"), "tp", None, None),
            P(("groups", "req"), None, "tp"),
            P(("groups", "req"), None, None),
        ),
        check_vma=False,
    )
```

```python
import functools

import jax
import jax.numpy as jnp
from jax import lax
from jax.experimental import pallas as pl
from jax.experimental.pallas import tpu as pltpu
from jax.sharding import PartitionSpec as P

HDIM = 64
STATE = 128
GHEADS = 32
CONV = 4
SPAN = 128
SUF = 512
INNER = 8192
BCG = 4
BCW = 1024
NCH = 4
LANES = 128
WIDE = 512
PIECE = 2
PROJ = 36
AHEAD = 3

F32 = jnp.float32
BF16 = jnp.bfloat16
HIGH = lax.Precision.HIGHEST


def wrap(x, n):
    return x & (n - 1) if n & (n - 1) == 0 else x % n


def over(x, n):
    return x >> (n.bit_length() - 1) if n & (n - 1) == 0 else x // n


def silu(x):
    half = 0.5 * x
    return half + half * jnp.tanh(half)


def split_pair(x, heads):
    lane = lax.broadcasted_iota(jnp.int32, x.shape, 1)
    high = x.astype(BF16).astype(F32)
    rest = jnp.where(lane < 2 * heads, x - high, 0.0)
    return jnp.where(lane < heads, high, rest).astype(BF16)


def dot(a, b):
    return jnp.dot(a, b, preferred_element_type=F32)


def dot_t(a, b):
    return lax.dot_general(a, b, (((1,), (1,)), ((), ())), preferred_element_type=F32)


def conv_taps(before, x, weight):
    extended = jnp.concatenate([before, x], axis=0)
    total = extended[8:] * weight[CONV - 1 :]
    for k in range(CONV - 1):
        total += extended[5 + k : 5 + k + SPAN] * weight[k : k + 1]
    return total


def pack_kernel(reqs, meta, px_ref, pb_ref, *conv_refs):
    slots = px_ref.shape[1]
    inner = px_ref.shape[2]
    me = meta[0]
    px = px_ref[...].astype(F32)
    pb = pb_ref[...].astype(F32)
    for by in range(reqs):
        at = jnp.clip(meta[2 + wrap(me + by, reqs)] - slots * me, 0, slots - 1)
        sent_x, sent_b = px[:, 0], pb[:, 0]
        for s in range(1, slots):
            sent_x = jnp.where(at == s, px[:, s], sent_x)
            sent_b = jnp.where(at == s, pb[:, s], sent_b)
        conv_refs[by][:, :inner] = sent_x.astype(BF16)
        conv_refs[by][:, inner:] = sent_b.astype(BF16)


def run_pack(meta, px, pb, reqs):
    taps, _, inner = px.shape
    return pl.pallas_call(
        functools.partial(pack_kernel, reqs),
        grid_spec=pltpu.PrefetchScalarGridSpec(
            num_scalar_prefetch=1,
            grid=(1,),
            in_specs=[
                pl.BlockSpec(px.shape, lambda i, m: (0, 0, 0)),
                pl.BlockSpec(pb.shape, lambda i, m: (0, 0, 0)),
            ],
            out_specs=[pl.BlockSpec((taps, inner + BCW), lambda i, m: (0, 0))] * reqs,
        ),
        out_shape=[jax.ShapeDtypeStruct((taps, inner + BCW), BF16)] * reqs,
        compiler_params=pltpu.CompilerParams(vmem_limit_bytes=8 * 2**20),
        cost_estimate=pl.CostEstimate(flops=10**6, bytes_accessed=2**18, transcendentals=0),
        name="pack",
    )(meta, px, pb)


def choose_kernel(reqs, slots, meta, mine_ref, mate_ref, out_ref, mark_ref):
    slot = meta[2 + wrap(meta[0] + 2 + 2 * pl.program_id(0), reqs)]
    out_ref[...] = jnp.where(over(slot, slots) == meta[0], mine_ref[...], mate_ref[...]).astype(BF16)
    mark_ref[...] = jnp.zeros_like(mark_ref)


def run_choose(meta, mine, mate, reqs):
    slots, inner, _ = mine.shape
    shape = (1, WIDE, STATE)

    def held(meta, by, owner):
        return jnp.clip(meta[2 + wrap(meta[0] + 2 + 2 * by, reqs)] - slots * owner, 0, slots - 1)

    return pl.pallas_call(
        functools.partial(choose_kernel, reqs, slots),
        grid_spec=pltpu.PrefetchScalarGridSpec(
            num_scalar_prefetch=1,
            grid=(reqs // 2 - 1, inner // WIDE),
            in_specs=[
                pl.BlockSpec(shape, lambda i, j, m: (held(m, i, m[0]), j, 0)),
                pl.BlockSpec(shape, lambda i, j, m: (held(m, i, m[0] ^ 1), j, 0)),
            ],
            out_specs=[
                pl.BlockSpec(shape, lambda i, j, m: (i, j, 0)),
                pl.BlockSpec((8, LANES), lambda i, j, m: (0, 0)),
            ],
        ),
        out_shape=[
            jax.ShapeDtypeStruct((reqs // 2 - 1, inner, STATE), BF16),
            jax.ShapeDtypeStruct((8, LANES), F32),
        ],
        compiler_params=pltpu.CompilerParams(vmem_limit_bytes=8 * 2**20),
        cost_estimate=pl.CostEstimate(flops=10**6, bytes_accessed=2 * 2**20, transcendentals=0),
        name="choose",
    )(meta, mine, mate)


def scan_kernel(
    heads,
    slots,
    reqs,
    meta,
    *refs,
):
    scan_body(heads, slots, reqs, meta, refs[:reqs], *refs[reqs + 1 :])


def scan_body(
    heads,
    slots,
    reqs,
    meta,
    conv_refs,
    x_ref,
    b_ref,
    c_ref,
    dt_ref,
    rate_ref,
    skip_ref,
    wx_ref,
    wb_ref,
    wc_ref,
    y_ref,
    final_ref,
    cmap_ref,
    reach_ref,
    total_ref,
    conv_ref,
    pick_ref,
    start,
    state,
    tail_x,
    tail_m,
    left,
    bmap_t,
    factors,
    base,
):
    block = pl.program_id(0)
    c = pl.program_id(1)
    me = meta[0]
    slot = meta[2 + me]
    inner = conv_ref.shape[1] - BCW
    wide = x_ref.shape[1]
    group = over(meta[1] * heads, GHEADS)

    @pl.when((block == 0) & (c == 0))
    def _():
        away = wrap(me - over(slot, slots) + reqs, reqs)
        taken = conv_refs[0][...].astype(F32)
        for by in range(1, reqs):
            taken = jnp.where(away == by, conv_refs[by][...].astype(F32), taken)
        taken = jnp.where(meta[2 + reqs + me] > 0, taken, 0.0)
        start[...] = jnp.concatenate(
            [jnp.zeros((8 - (CONV - 1), inner + BCW), F32), taken], axis=0
        )
        conv_ref[...] = taken.astype(BF16)

    @pl.when(block == 0)
    def _():
        maps = []
        for k, (ref, w) in enumerate(((b_ref, wb_ref), (c_ref, wc_ref))):
            at = pl.multiple_of(inner + (group + k * BCG) * LANES, LANES)
            before = jnp.where(c == 0, start[:, pl.ds(at, LANES)], tail_m[k])
            x = ref[...].astype(F32)
            maps.append(silu(conv_taps(before, x, w[...].astype(F32))).astype(BF16))
            tail_m[k] = x[SPAN - 8 :]
        bmap, cmap = maps
        row = lax.broadcasted_iota(jnp.int32, (SPAN, SPAN), 0)
        col = lax.broadcasted_iota(jnp.int32, (SPAN, SPAN), 1)
        scores = jnp.where(row >= col, dot_t(cmap, bmap), 0.0).astype(BF16)
        left[c, :, :SPAN] = scores
        left[c, :, SPAN:] = cmap
        cmap_ref[...] = cmap
        bmap_t[c] = jnp.transpose(bmap.astype(F32)).astype(BF16)

        @pl.when(c == 0)
        def _():
            base[...] = jnp.zeros_like(base)

        copies = LANES // heads
        logit = jnp.transpose(jnp.concatenate([dt_ref[...]] * copies, axis=0))
        rate = jnp.concatenate([rate_ref[...].reshape(1, heads)] * copies, axis=1)
        skip = jnp.concatenate([skip_ref[...].reshape(1, heads)] * copies, axis=1)
        live = (row + c * SPAN < meta[2 + 3 * reqs + me]).astype(F32)
        step = (jnp.maximum(logit, 0.0) + jnp.log1p(jnp.exp(-jnp.abs(logit)))) * live
        cum = jnp.dot(
            (row >= col).astype(F32),
            -step * rate,
            precision=HIGH,
            preferred_element_type=F32,
        )
        last = cum[SPAN - 1 :]
        mid = 0.5 * last
        factors[c, :SPAN] = split_pair(jnp.exp(cum - mid), heads)
        factors[c, SPAN : 2 * SPAN] = split_pair(jnp.exp(mid - cum) * step, heads)
        before = base[0:1]
        reach_ref[...] = split_pair(jnp.exp(before + cum), heads)
        which = lax.broadcasted_iota(jnp.int32, (16, LANES), 0)
        singles = jnp.where(which == 1, jnp.exp(last - mid), skip)
        factors[c, 2 * SPAN :] = split_pair(jnp.where(which == 0, jnp.exp(mid), singles), heads)
        base[...] = base[...] + last
        total_ref[...] = split_pair(jnp.exp(base[...]), heads)

    @pl.when(c == 0)
    def _():
        state[...] = jnp.zeros_like(state)
        lane = lax.broadcasted_iota(jnp.int32, (LANES, wide), 0)
        channel = lax.broadcasted_iota(jnp.int32, (LANES, wide), 1) + block * wide
        pick_ref[...] = ((wrap(lane, heads) == over(channel, HDIM)) & (lane < 2 * heads)).astype(BF16)
        tail_x[...] = start[:, pl.ds(pl.multiple_of(block * wide, wide), wide)]

    x = x_ref[...].astype(F32)
    conv = conv_taps(tail_x[...], x, wx_ref[...].astype(F32))
    tail_x[...] = x[SPAN - 8 :]
    values = silu(conv).astype(BF16).astype(F32)
    spread = dot(factors[c], pick_ref[...])
    rows = spread[2 * SPAN :]
    scaled = (values * spread[SPAN : 2 * SPAN]).astype(BF16)
    held = state[...] * rows[0:1]
    right = jnp.concatenate([scaled, held.astype(BF16)], axis=0)
    y_ref[...] = (dot(left[c], right) * spread[:SPAN] + rows[2:3] * values).astype(BF16)
    state[...] = (held + dot(bmap_t[c], scaled)) * rows[1:2]

    @pl.when(c == NCH - 1)
    def _():
        final_ref[...] = jnp.transpose(state[...]).astype(BF16)


def run_scan(meta, conv, mark, x, bc, dt, rate, skip, wx, wbc, heads, slots):
    inner = x.shape[1]
    wide = min(2048, inner)
    blocks = inner // wide
    reqs = len(conv)
    once = lambda b, c: jnp.where(b == 0, c, NCH - 1)
    group = lambda m: over(m[1] * heads, GHEADS)
    in_specs = [pl.BlockSpec((CONV - 1, inner + BCW), lambda b, c, m: (0, 0))] * reqs
    in_specs += [
        pl.BlockSpec((8, LANES), lambda b, c, m: (0, 0)),
        pl.BlockSpec((SPAN, wide), lambda b, c, m: (c, b)),
        pl.BlockSpec((SPAN, LANES), lambda b, c, m: (once(b, c), group(m))),
        pl.BlockSpec((SPAN, LANES), lambda b, c, m: (once(b, c), group(m) + BCG)),
        pl.BlockSpec((heads, SPAN), lambda b, c, m: (0, once(b, c))),
        pl.BlockSpec((heads,), lambda b, c, m: (0,)),
        pl.BlockSpec((heads,), lambda b, c, m: (0,)),
        pl.BlockSpec((CONV, wide), lambda b, c, m: (0, b)),
        pl.BlockSpec((CONV, LANES), lambda b, c, m: (0, group(m))),
        pl.BlockSpec((CONV, LANES), lambda b, c, m: (0, group(m) + BCG)),
    ]
    out_specs = [
        pl.BlockSpec((SPAN, wide), lambda b, c, m: (c, b)),
        pl.BlockSpec((wide, STATE), lambda b, c, m: (b, 0)),
        pl.BlockSpec((SPAN, LANES), lambda b, c, m: (once(b, c), 0)),
        pl.BlockSpec((SPAN, LANES), lambda b, c, m: (once(b, c), 0)),
        pl.BlockSpec((16, LANES), lambda b, c, m: (0, 0)),
        pl.BlockSpec((CONV - 1, inner + BCW), lambda b, c, m: (0, 0)),
        pl.BlockSpec((LANES, wide), lambda b, c, m: (0, b)),
    ]
    return pl.pallas_call(
        functools.partial(scan_kernel, heads, slots, reqs),
        grid_spec=pltpu.PrefetchScalarGridSpec(
            num_scalar_prefetch=1,
            grid=(blocks, NCH),
            in_specs=in_specs,
            out_specs=out_specs,
            scratch_shapes=[
                pltpu.VMEM((8, inner + BCW), F32),
                pltpu.VMEM((STATE, wide), F32),
                pltpu.VMEM((8, wide), F32),
                pltpu.VMEM((2, 8, LANES), F32),
                pltpu.VMEM((NCH, SPAN, 2 * SPAN), BF16),
                pltpu.VMEM((NCH, STATE, SPAN), BF16),
                pltpu.VMEM((NCH, 2 * SPAN + 16, LANES), BF16),
                pltpu.VMEM((16, LANES), F32),
            ],
        ),
        out_shape=[
            jax.ShapeDtypeStruct((SUF, inner), BF16),
            jax.ShapeDtypeStruct((inner, STATE), BF16),
            jax.ShapeDtypeStruct((SUF, LANES), BF16),
            jax.ShapeDtypeStruct((SUF, LANES), BF16),
            jax.ShapeDtypeStruct((16, LANES), BF16),
            jax.ShapeDtypeStruct((CONV - 1, inner + BCW), BF16),
            jax.ShapeDtypeStruct((LANES, inner), BF16),
        ],
        compiler_params=pltpu.CompilerParams(
            dimension_semantics=("arbitrary", "arbitrary"), vmem_limit_bytes=16 * 2**20
        ),
        cost_estimate=pl.CostEstimate(
            flops=8 * 10**9, bytes_accessed=12 * 2**20, transcendentals=SUF * inner
        ),
        name="local_scan",
    )(meta, *conv, mark, x, bc, bc, dt, rate, skip, wx, wbc, wbc)


def project_kernel(chunks, shares, picks, emit, late, meta, *refs):
    if picks:
        reqs, slots = picks
        others = reqs // 2 - 1
        mine_ref, mate_ref = refs[:2]
        got_refs = refs[2 : 2 + others]
        refs = refs[2 + others :]
    else:
        start_ref, refs = refs[0], refs[1:]
    y_ref, gate_ref, cmap_ref, reach_ref, gain_ref, pick_ref, w_ref = refs[:7]
    out_refs = refs[7 : 7 + len(emit)]
    late_refs = refs[7 + len(emit) : 7 + len(emit) + len(late)]
    refs = refs[7 + len(emit) + len(late) :]
    sq_ref = refs[0]
    if picks:
        start_ref = refs[1]
    held, w_held, arrived = refs[-3:]
    step = pl.program_id(0)
    inner = y_ref.shape[1]
    share = out_refs[0].shape[1]

    def fetch(i):
        q = emit[i]
        to = jnp.where(2 * meta[1] < shares, meta[1] + q, meta[1] - q + shares)
        column = pl.multiple_of(wrap(to, shares) * share, share)
        return pltpu.make_async_copy(
            w_ref.at[:, pl.ds(column, share)], w_held.at[i % AHEAD], arrived.at[i % AHEAD]
        )

    @pl.when(step == 0)
    def _():
        for i in range(min(AHEAD, len(emit))):
            fetch(i).start()

    if picks:

        @pl.when(step == 0)
        def _():
            me = meta[0]
            owner = over(meta[2 + me], slots)
            away = wrap(over(me, 2) - over(owner, 2) + reqs // 2, reqs // 2)
            taken = jnp.where(owner == me, mine_ref[0], mate_ref[0])
            for k in range(others):
                taken = jnp.where(away == k + 1, got_refs[k][0].astype(F32), taken)
            start_ref[...] = jnp.where(meta[2 + reqs + me] > 0, taken, 0.0).astype(BF16)

    @pl.when(step < chunks)
    def _():
        squares = jnp.zeros((SPAN, LANES), F32)
        rows = pl.ds(pl.multiple_of(step * SPAN, SPAN), SPAN)
        for i in range(inner // WIDE):
            at = pl.ds(i * WIDE, WIDE)
            carried = dot_t(cmap_ref[...], start_ref[at, :])
            y = y_ref[:, at].astype(F32) + dot(reach_ref[...], pick_ref[:, at]) * carried
            gated = y * silu(gate_ref[:, at].astype(F32))
            held[rows, at] = (gated * gain_ref[:, at]).astype(BF16)
            gated = gated * gated
            for j in range(WIDE // LANES):
                squares += gated[:, j * LANES : (j + 1) * LANES]
        sq_ref[...] = lax.dot_general(
            jnp.ones((8, LANES), F32),
            squares,
            (((1,), (1,)), ((), ())),
            precision=HIGH,
            preferred_element_type=F32,
        )

    for i in range(len(emit)):

        @pl.when(step == chunks + i)
        def _(i=i):
            fetch(i).wait()
            done = held.shape[0] - out_refs[i].shape[0]
            out_refs[i][...] = dot(held[done:], w_held[i % AHEAD]).astype(BF16)
            if emit[i] in late:
                late_refs[late.index(emit[i])][...] = dot(
                    held[:done], w_held[i % AHEAD]
                ).astype(BF16)
            if i + AHEAD < len(emit):
                fetch(i + AHEAD).start()


def run_project(
    done, chunks, emit, late, meta, states, y, gate, cmap, reach, gain, pick, weight, shares, reqs
):
    inner, width = weight.shape
    share = width // shares
    count = (chunks - done) * SPAN
    rows = lambda n, m: (jnp.minimum(n, chunks - 1), 0)
    whole = lambda n, m: (0, 0)
    state = (1, inner, STATE)
    choose = len(states) > 1
    single = pl.Buffered(1)
    slots = states[0].shape[0]

    def held(owner, m):
        return jnp.clip(m[2 + m[0]] - slots * owner, 0, slots - 1)

    if choose:
        state_specs = [
            pl.BlockSpec(state, lambda n, m: (held(m[0], m), 0, 0), pipeline_mode=single),
            pl.BlockSpec(state, lambda n, m: (held(m[0] ^ 1, m), 0, 0), pipeline_mode=single),
        ] + [pl.BlockSpec(state, lambda n, m: (0, 0, 0), pipeline_mode=single)] * (len(states) - 2)
    else:
        state_specs = [pl.BlockSpec((inner, STATE), whole, pipeline_mode=single)]
    out_specs = [
        pl.BlockSpec((count, share), whole)
        for q in emit
    ]
    out_specs += [pl.BlockSpec((done * SPAN, share), whole) for q in late]
    out_specs += [pl.BlockSpec((8, LANES), lambda n, m: (0, jnp.minimum(n, chunks - 1)))]
    out_shape = [jax.ShapeDtypeStruct((count, share), BF16)] * len(emit)
    out_shape += [jax.ShapeDtypeStruct((done * SPAN, share), BF16)] * len(late)
    out_shape.append(jax.ShapeDtypeStruct((8, chunks * SPAN), F32))
    if choose:
        out_specs.append(pl.BlockSpec((inner, STATE), whole))
        out_shape.append(jax.ShapeDtypeStruct((inner, STATE), BF16))
    return pl.pallas_call(
        functools.partial(project_kernel, chunks, shares, (reqs, slots) if choose else None, emit, late),
        grid_spec=pltpu.PrefetchScalarGridSpec(
            num_scalar_prefetch=1,
            grid=(chunks + len(emit),),
            in_specs=state_specs
            + [
                pl.BlockSpec((SPAN, inner), rows),
                pl.BlockSpec((SPAN, inner), rows),
                pl.BlockSpec((SPAN, LANES), rows),
                pl.BlockSpec((SPAN, LANES), rows),
                pl.BlockSpec((1, inner), whole),
                pl.BlockSpec((LANES, inner), whole, pipeline_mode=single),
                pl.BlockSpec(memory_space=pl.ANY),
            ],
            out_specs=out_specs,
            scratch_shapes=[
                pltpu.VMEM((chunks * SPAN, inner), BF16),
                pltpu.VMEM((AHEAD, inner, share), BF16),
                pltpu.SemaphoreType.DMA((AHEAD,)),
            ],
        ),
        out_shape=out_shape,
        compiler_params=pltpu.CompilerParams(
            dimension_semantics=("arbitrary",), vmem_limit_bytes=PROJ * 2**20
        ),
        cost_estimate=pl.CostEstimate(flops=1, bytes_accessed=1, transcendentals=0),
        name="project",
    )(meta, *states, y, gate, cmap, reach, gain, pick, weight)


def line_sums(parts, mark, size):
    parts = list(parts)
    sums = []
    for p in range(len(parts)):
        landed = []
        came = {}
        for k in range(size - 1):
            for d in range(size - 1, k, -1):
                slot = d - k if 2 * k < size else size - d + k
                go = parts[p][slot]
                if k:
                    go = (go.astype(F32) + came[k - 1, d].astype(F32)).astype(BF16)
                came[k, d] = lax.ppermute(
                    go, "tp", [(k, k + 1), (size - 1 - k, size - 2 - k)]
                )
                if k == 0 and d == size - 1 and p + 1 < len(parts):
                    came[k, d], parts[p + 1], mark = lax.optimization_barrier(
                        (came[k, d], parts[p + 1], mark)
                    )
            landed.append(came[k, k + 1])
        total = parts[p][0].astype(F32)
        for value in landed:
            total += value.astype(F32)
        sums.append(total)
    return mark, sums


def source_of(meta, device, reqs):
    found = jnp.int32(0)
    for r in range(reqs):
        found += jnp.where(meta[2 + 2 * reqs + r] == device, r, 0)
    return found


def ending_kernel(reqs, meta, mark_ref, local_ref, start_ref, total_ref, pick_ref, conv_ref, x_ref, bc_ref, out_ref):
    inner = local_ref.shape[0]
    length = meta[2 + 3 * reqs + meta[0]]
    for i in range(inner // WIDE):
        at = pl.ds(i * WIDE, WIDE)
        decay = dot(total_ref[...], pick_ref[:, at])[0:1]
        decay = jnp.transpose(jnp.broadcast_to(decay, (STATE, WIDE)))
        out_ref[at, :] = (local_ref[at, :].astype(F32) + decay * start_ref[at, :].astype(F32)).astype(BF16)
    row = lax.broadcasted_iota(jnp.int32, (16, SUF), 0) + length - (CONV - 1)
    found = (row == lax.broadcasted_iota(jnp.int32, (16, SUF), 1)).astype(BF16)
    conv = conv_ref[...].astype(F32)
    row = lax.broadcasted_iota(jnp.int32, (16, WIDE), 0) + length
    for i in range((inner + BCW) // WIDE):
        at = i * WIDE
        source = x_ref[:, at : at + WIDE] if at < inner else bc_ref[:, at - inner : at - inner + WIDE]
        tail = dot(found, source)
        for k in range(CONV - 1):
            tail += jnp.where(row == k, conv[k : k + 1, at : at + WIDE], 0.0)
        tail = tail.astype(BF16)
        for j in range(WIDE // LANES):
            to = inner + (at // LANES + j) * 16
            out_ref[to : to + 16, :] = tail[:, j * LANES : (j + 1) * LANES]


def run_ending(meta, mark, local, start, total, pick, conv, x, bc, reqs):
    inner = local.shape[0]
    rows = inner + (inner + BCW) // LANES * 16
    operands = (mark, local, start, total, pick, conv, x, bc)
    return pl.pallas_call(
        functools.partial(ending_kernel, reqs),
        grid_spec=pltpu.PrefetchScalarGridSpec(
            num_scalar_prefetch=1,
            grid=(1,),
            in_specs=[pl.BlockSpec(a.shape, lambda i, m: (0, 0)) for a in operands],
            out_specs=pl.BlockSpec((rows, LANES), lambda i, m: (0, 0)),
        ),
        out_shape=jax.ShapeDtypeStruct((rows, LANES), BF16),
        compiler_params=pltpu.CompilerParams(vmem_limit_bytes=16 * 2**20),
        cost_estimate=pl.CostEstimate(flops=1, bytes_accessed=1, transcendentals=0),
        name="ending",
    )(meta, *operands)


def route_kernel(reqs, meta, *refs):
    origin = over(source_of(meta, meta[0] ^ 1, reqs), 2)
    away = wrap(over(meta[0], 2) - origin + reqs // 2, reqs // 2)
    taken = refs[0][...]
    for k in range(1, reqs // 2):
        taken = jnp.where(away == k, refs[k][...], taken)
    refs[-1][...] = taken


def run_route(meta, ends, reqs):
    shape = ends[0].shape
    return pl.pallas_call(
        functools.partial(route_kernel, reqs),
        grid_spec=pltpu.PrefetchScalarGridSpec(
            num_scalar_prefetch=1,
            grid=(1,),
            in_specs=[pl.BlockSpec(shape, lambda i, m: (0, 0))] * len(ends),
            out_specs=pl.BlockSpec(shape, lambda i, m: (0, 0)),
        ),
        out_shape=jax.ShapeDtypeStruct(shape, BF16),
        compiler_params=pltpu.CompilerParams(vmem_limit_bytes=12 * 2**20),
        cost_estimate=pl.CostEstimate(flops=1, bytes_accessed=1, transcendentals=0),
        name="route",
    )(meta, *ends)


def land_kernel(reqs, meta, *refs):
    state_ref, x_ref, bc_ref = refs[-3:]
    crossed_ref = refs[-4]
    source = source_of(meta, meta[0], reqs)
    away = wrap(over(meta[0], 2) - over(source, 2) + reqs // 2, reqs // 2)
    inner = state_ref.shape[0]

    def taken(at):
        value = refs[0][at, :]
        for k in range(1, reqs // 2):
            value = jnp.where(away == k, refs[k][at, :], value)
        return jnp.where((source & 1) == (meta[0] & 1), value, crossed_ref[at, :])

    for i in range(inner // WIDE):
        at = pl.ds(i * WIDE, WIDE)
        state_ref[at, :] = taken(at).astype(F32)
    tiles = (inner + BCW) // LANES
    tails = [taken(pl.ds(inner + j * 16, 16))[: CONV - 1] for j in range(tiles)]
    x_ref[...] = jnp.concatenate(tails[: inner // LANES], axis=1)
    bc_ref[...] = jnp.concatenate(tails[inner // LANES :], axis=1)


def run_land(meta, ends, crossed, inner, reqs):
    shape = crossed.shape
    outs = [(inner, STATE), (CONV - 1, inner), (CONV - 1, BCW)]
    return pl.pallas_call(
        functools.partial(land_kernel, reqs),
        grid_spec=pltpu.PrefetchScalarGridSpec(
            num_scalar_prefetch=1,
            grid=(1,),
            in_specs=[pl.BlockSpec(shape, lambda i, m: (0, 0))] * (len(ends) + 1),
            out_specs=[pl.BlockSpec(o, lambda i, m: (0, 0)) for o in outs],
        ),
        out_shape=[jax.ShapeDtypeStruct(o, t) for o, t in zip(outs, (F32, BF16, BF16))],
        compiler_params=pltpu.CompilerParams(vmem_limit_bytes=16 * 2**20),
        cost_estimate=pl.CostEstimate(flops=1, bytes_accessed=1, transcendentals=0),
        name="land",
    )(meta, *ends, crossed)


def shifted(x, axis, size, by):
    return lax.ppermute(x, axis, [(i, (i + by) % size) for i in range(size)])


def swap_core(x, size):
    return lax.ppermute(x, "req", [(i, i ^ 1) for i in range(size)])


def per_device(
    ssm_input,
    gate_input,
    bc_input,
    dt_input,
    decay_rate,
    skip_gain,
    norm_gain,
    conv_x_weight,
    conv_bc_weight,
    out_weight,
    pool_states,
    pool_conv_x,
    pool_conv_bc,
    prefix_slot,
    prefix_spans,
    dest_slot,
    suffix_len,
):
    num_req = lax.axis_size("req")
    num_tp = lax.axis_size("tp")
    me = lax.axis_index("req")
    z = lax.axis_index("tp")
    heads = dt_input.shape[1]
    inner = ssm_input.shape[1]
    slots = pool_states.shape[0]
    meta = jnp.concatenate(
        [jnp.stack([me, z]), prefix_slot, prefix_spans, dest_slot, suffix_len]
    ).astype(jnp.int32)

    mine = pool_states.reshape(slots, inner, STATE)
    other = swap_core(mine, num_req)
    conv = run_pack(
        meta,
        jnp.transpose(pool_conv_x, (1, 0, 2)),
        jnp.transpose(pool_conv_bc, (1, 0, 2)),
        num_req,
    )
    chosen, mark = run_choose(meta, mine, other, num_req)
    convs = [conv[0]] + [shifted(conv[by], "req", num_req, by) for by in range(1, num_req)]
    got = [
        shifted(chosen[k : k + 1], "req", num_req, 2 * k + 2) for k in range(num_req // 2 - 1)
    ]

    y_local, local_final, cmap, reach, total, start_conv, pick = run_scan(
        meta,
        convs,
        mark,
        ssm_input,
        bc_input,
        dt_input.T,
        decay_rate,
        skip_gain,
        conv_x_weight,
        conv_bc_weight,
        heads,
        slots,
    )
    states = [mine, other] + got
    operands = (y_local, gate_input, cmap, reach, norm_gain[None, :], pick, out_weight, num_tp, num_req)
    soon, rest = (num_tp - 1, num_tp - 2), tuple(range(num_tp - 2))
    first = run_project(0, PIECE, soon, (), meta, [mine, other] + got, *operands)
    start = first[3]
    second = list(run_project(PIECE, NCH, rest + soon, rest, meta, [start], *operands))
    parts = [second[num_tp : num_tp + len(rest)] + [first[1], first[0]], list(second[: len(rest)])]
    parts[1] += [second[num_tp - 1], second[num_tp - 2]]
    parts = [tuple(part) for part in parts]
    result = {num_tp: second[-1]}
    mark, summed = line_sums(parts, result[num_tp], num_tp)
    summed = jnp.concatenate(summed, axis=0)

    my_len = suffix_len[me]
    square = second[-1][0]
    square_total = square
    for by in range(1, num_tp):
        square_total = square_total + shifted(square, "tp", num_tp, by)
    scale = lax.rsqrt(square_total / INNER + 1e-05)
    scale = jnp.where(jnp.arange(SUF) < my_len, scale, 0.0)
    mixed = (summed * scale[:, None]).astype(BF16)

    end = run_ending(
        meta, mark, local_final, start, total, pick, start_conv, ssm_input, bc_input, num_req
    )
    ends = [end] + [shifted(end, "req", num_req, by) for by in range(2, num_req, 2)]
    crossed = swap_core(run_route(meta, ends, num_req), num_req)
    ckpt_states, ckpt_x, ckpt_bc = run_land(meta, ends, crossed, inner, num_req)
    return (
        mixed,
        ckpt_states.reshape((1, heads, HDIM, STATE)),
        ckpt_x[None],
        ckpt_bc[None],
    )


def solution(mesh):
    return jax.shard_map(
        per_device,
        mesh=mesh,
        in_specs=(
            P(("groups", "req"), "tp"),
            P(("groups", "req"), "tp"),
            P(("groups", "req"), None),
            P(("groups", "req"), "tp"),
            P("tp"),
            P("tp"),
            P("tp"),
            P(None, "tp"),
            P(),
            P("tp", None),
            P(("groups", "req"), "tp", None, None),
            P(("groups", "req"), None, "tp"),
            P(("groups", "req"), None, None),
            P("groups"),
            P("groups"),
            P("groups"),
            P("groups"),
        ),
        out_specs=(
            P(("groups", "req"), "tp"),
            P(("groups", "req"), "tp", None, None),
            P(("groups", "req"), None, "tp"),
            P(("groups", "req"), None, None),
        ),
        check_vma=False,
    )
```
